32 devices in a mesh: sub: 4 (over z), cgrp: 8 (over y, x, core).
Axes of the slice: x: 2, y: 2, z: 4, core: 2. Of those that a mesh axis runs over, the one named last changes fastest.
Arguments:
- source: float32 [256, 32768], P('sub', 'cgrp'), may hold values from -7.5 to 7.5
- capacity: float32 [256, 32768], P('sub', 'cgrp'), may hold values from 0.01 to 1
- fd_weights: float32 [256, 32768], P('sub', 'cgrp'), may hold values from 0.02 to 1
- fd_modes: float32 [3, 64, 64], replicated, may hold values from -0.75 to 0.75
- face_modes: float32 [2, 128, 64], replicated, may hold values from -0.75 to 0.75
- coarse_map: int32 [4, 8, 6, 128], P('sub', 'cgrp'), may hold values from 0 to 24575, as said below
- fsai_cols: int32 [192, 8], P(('sub', 'cgrp')), may hold values from 0 to 191
- fsai_blocks: float32 [192, 8, 128, 128], P(('sub', 'cgrp')), may hold values from -0.1875 to 0.1875
Outputs:
- solution: float32 [256, 32768], P('sub', 'cgrp')
- residual: float32 [256, 32768], P('sub', 'cgrp')
The draws below stay inside these ranges and needn't reach their ends.
Inputs may be any that keep to these rules, and one draw needn't show every extreme that they name: `coarse_map`: entries are numbered by owner: with d = s * 8 + t, face f of subdomain (s, t) takes the entries (6 d + f) * 128 to (6 d + f) * 128 + 127, each once, in an order of its own; except that face 0 of a subdomain with s > 0 takes exactly the entries of face 1 of subdomain (s - 1, t), and face 2 of a subdomain with t > 0 exactly those of face 3 of subdomain (s, t - 1), function k of both sides taking the same entry.
All inputs are finite; a program needn't handle non-finite values.
Results may differ from the reference program's by a relative error of at most 0.0001.
Values sent between devices are 32-bit elements; how exact they have to be, the bound alone decides.
A program may use at most 64 MiB of HBM per device.

```python
import math
import jax
import jax.numpy as jnp
from jax import lax

C = 64
CF = 128
BS = 128
NNZB = 8
ITERS = 1
SDX = 4
SDY = 8
NX = 256
NY = 512
NZ = 64
NCOARSE = 24576
NBLK = 192


def draw_source(key, part):
    ramp = 1.0 + 2.0 * jnp.arange(NX, dtype=jnp.float32) / (NX - 1)
    field = ramp[:, None, None] * jnp.clip(jax.random.normal(key, (NX, NY, NZ), jnp.float32), -2.5, 2.5)
    return field.reshape(NX, NY * NZ)


def draw_coarse_map(key, part):
    first = jnp.arange(SDX, dtype=jnp.int32)[:, None] * jnp.ones((1, SDY), jnp.int32)
    second = jnp.ones((SDX, 1), jnp.int32) * jnp.arange(SDY, dtype=jnp.int32)[None, :]
    device = first * SDY + second
    inner_first = (first > 0).astype(jnp.int32)
    inner_second = (second > 0).astype(jnp.int32)
    low_first = (device - SDY * inner_first) * 6 + inner_first
    low_second = (device - inner_second) * 6 + 2 + inner_second
    owners = jnp.stack([low_first, device * 6 + 1, low_second, device * 6 + 3, device * 6 + 4, device * 6 + 5], axis=-1)
    scores = jax.random.randint(key, (SDX * SDY * 6, CF), 0, 2 ** 20) * CF
    scores = scores + jnp.arange(CF, dtype=jnp.int32)[None, :]
    order = jnp.argsort(scores, axis=1).astype(jnp.int32)
    return (owners[..., None] * CF + order[owners]).astype(jnp.int32)


def set_ends(result, own_key, smallest, largest):
    longest = result.shape.index(max(result.shape))
    spots = []
    for shift in (0, 1):
        where = [jax.random.randint(jax.random.fold_in(own_key, axis), (), 0, length) for axis, length in enumerate(result.shape)]
        where[longest] = (where[longest] + shift) % result.shape[longest]
        spots.append(tuple(where))
    return result.at[spots[0]].set(smallest).at[spots[1]].set(largest)


def level_of(rng, dims, shards, smallest, high):
    loudness, own = 1.0, jax.random.fold_in(rng, 6)
    for axis_at, shards_of in shards:
        heights = jnp.exp(jax.random.uniform(jax.random.fold_in(own, axis_at), (shards_of,), jnp.float32, smallest / len(shards), high / len(shards)))
        loudness = loudness * jnp.repeat(heights, dims[axis_at] // shards_of).reshape([-1 if axis == axis_at else 1 for axis in range(len(dims))])
    return loudness


def normal_values(rng, dims, scale, limit, pieces=(), kind=jnp.bfloat16):
    array = jax.random.normal(rng, dims, jnp.float32) * scale
    if len(pieces) > 0:
        array = level_of(rng, dims, pieces, -0.22, 0.18) * array
    return jnp.clip(array, min=-limit, max=limit).astype(kind)


def setup_inputs(seed: int = 0) -> dict:
    streams_of = jax.random.split(jax.random.key(seed), 9)
    source = draw_source(jax.random.fold_in(streams_of[8], 71), 0)
    capacity = jnp.clip(jnp.exp(math.log(1.0) - 4.6051702 * jax.random.uniform(streams_of[1], (NX, NY * NZ), jnp.float32) ** level_of(streams_of[1], (NX, NY * NZ), ((0, 4), (1, 8)), -0.2, 0.2)), 0.01, 1.0)
    fd_weights = jnp.clip(jnp.exp(math.log(1.0) - 3.912023 * jax.random.uniform(streams_of[2], (NX, NY * NZ), jnp.float32) ** level_of(streams_of[2], (NX, NY * NZ), ((0, 4), (1, 8)), -0.2, 0.2)), 0.02, 1.0)
    fd_modes = normal_values(streams_of[3], (3, C, C), C ** -0.5, 0.75, (), jnp.float32)
    face_modes = normal_values(streams_of[4], (2, CF, C), (CF // 2) ** -0.5, 0.75, (), jnp.float32)
    coarse_map = draw_coarse_map(jax.random.fold_in(streams_of[8], 71), 0)
    fsai_cols = set_ends(jax.random.randint(streams_of[6], (NBLK, NNZB), 0, NBLK), jax.random.fold_in(streams_of[6], 1), 0, NBLK - 1).astype(jnp.int32)
    fsai_blocks = normal_values(streams_of[7], (NBLK, NNZB, BS, BS), (NNZB * BS) ** -0.5, 0.1875, ((0, 32),), jnp.float32)
    return dict(source=source, capacity=capacity, fd_weights=fd_weights, fd_modes=fd_modes, face_modes=face_modes, coarse_map=coarse_map, fsai_cols=fsai_cols, fsai_blocks=fsai_blocks)


highest = lax.Precision.HIGHEST
along_first = 1.0
along_second = 0.6
along_third = 2.5


def operate(field, capacity):
    padded = jnp.pad(field, 1)
    first = padded[2:, 1:-1, 1:-1] + padded[:-2, 1:-1, 1:-1]
    second = padded[1:-1, 2:, 1:-1] + padded[1:-1, :-2, 1:-1]
    third = padded[1:-1, 1:-1, 2:] + padded[1:-1, 1:-1, :-2]
    diagonal = capacity + 2.0 * (along_first + along_second + along_third)
    return diagonal * field - along_first * first - along_second * second - along_third * third


def to_blocks(field):
    return field.reshape(SDX, C, SDY, C, C).transpose(0, 2, 1, 3, 4)


def from_blocks(blocks):
    return blocks.transpose(0, 2, 1, 3, 4).reshape(NX, NY, NZ)


def transform(blocks, modes):
    blocks = jnp.einsum('ai,...ijk->...ajk', modes[0], blocks, precision=highest)
    blocks = jnp.einsum('bj,...ajk->...abk', modes[1], blocks, precision=highest)
    return jnp.einsum('ck,...abk->...abc', modes[2], blocks, precision=highest)


def transform_back(blocks, modes):
    blocks = jnp.einsum('ai,...ajk->...ijk', modes[0], blocks, precision=highest)
    blocks = jnp.einsum('bj,...ibk->...ijk', modes[1], blocks, precision=highest)
    return jnp.einsum('ck,...ijc->...ijk', modes[2], blocks, precision=highest)


def face_planes(blocks):
    return jnp.stack([blocks[..., 0, :, :], blocks[..., -1, :, :], blocks[..., :, 0, :],
                      blocks[..., :, -1, :], blocks[..., :, :, 0], blocks[..., :, :, -1]], axis=-3)


def restrict(planes, face_modes):
    partial_rows = jnp.einsum('ka,...fab->...fkb', face_modes[0], planes, precision=highest)
    return jnp.sum(partial_rows * face_modes[1], axis=-1)


def extend(values, face_modes):
    return jnp.einsum('ka,...fkb->...fab', face_modes[0], values[..., None] * face_modes[1], precision=highest)


def add_planes(blocks, planes):
    blocks = blocks.at[..., 0, :, :].add(planes[..., 0, :, :])
    blocks = blocks.at[..., -1, :, :].add(planes[..., 1, :, :])
    blocks = blocks.at[..., :, 0, :].add(planes[..., 2, :, :])
    blocks = blocks.at[..., :, -1, :].add(planes[..., 3, :, :])
    blocks = blocks.at[..., :, :, 0].add(planes[..., 4, :, :])
    blocks = blocks.at[..., :, :, -1].add(planes[..., 5, :, :])
    return blocks


def coarse_apply(coarse, fsai_cols, fsai_blocks):
    table = coarse.reshape(-1, fsai_blocks.shape[2])
    picked = table[fsai_cols]
    image = jnp.einsum('rnij,rnj->ri', fsai_blocks, picked, precision=highest)
    spread = jnp.einsum('rnij,ri->rnj', fsai_blocks, image, precision=highest)
    return jnp.zeros_like(table).at[fsai_cols].add(spread).reshape(-1)


def precondition(residual, fd_weights, fd_modes, face_modes, coarse_map, fsai_cols, fsai_blocks):
    blocks = to_blocks(residual)
    local = transform_back(to_blocks(fd_weights) * transform(blocks, fd_modes), fd_modes)
    coarse_local = restrict(face_planes(blocks), face_modes)
    slots = coarse_map.reshape(-1).astype(jnp.int32)
    coarse = jnp.zeros((NCOARSE,), jnp.float32).at[slots].add(coarse_local.reshape(-1))
    back = coarse_apply(coarse, fsai_cols, fsai_blocks)
    correction = back[slots].reshape(coarse_local.shape)
    return from_blocks(add_planes(local, extend(correction, face_modes)))


def reference(source, capacity, fd_weights, fd_modes, face_modes, coarse_map, fsai_cols, fsai_blocks):
    source = source.reshape(NX, NY, NZ)
    capacity = capacity.reshape(NX, NY, NZ)
    fd_weights = fd_weights.reshape(NX, NY, NZ)

    def precond_of(vector):
        return precondition(vector, fd_weights, fd_modes, face_modes, coarse_map, fsai_cols, fsai_blocks)

    solution = jnp.zeros_like(source)
    residual = source
    precond = precond_of(residual)
    direction = precond
    gamma = jnp.sum(residual * precond)
    for step in range(ITERS):
        image = operate(direction, capacity)
        alpha = gamma / jnp.sum(direction * image)
        solution = solution + alpha * direction
        residual = residual - alpha * image
        if step + 1 < ITERS:
            precond = precond_of(residual)
            gamma_next = jnp.sum(residual * precond)
            direction = precond + (gamma_next / gamma) * direction
            gamma = gamma_next
    flat = (NX, NY * NZ)
    return solution.reshape(flat), residual.reshape(flat)
```

```python
import functools
import jax
import jax.numpy as jnp
from jax import lax
from jax.experimental import pallas as pl
from jax.experimental.pallas import tpu as pltpu
from jax.sharding import PartitionSpec as P

C = 64
T = 32
CH = 8
f32 = jnp.float32
bf16 = jnp.bfloat16
HI = lax.Precision.HIGHEST
MESH = pl.DeviceIdType.MESH


def nn(a, b):
    return lax.dot_general(a, b, (((1,), (0,)), ((), ())), precision=HI, preferred_element_type=f32)


def nt(a, b):
    return lax.dot_general(a, b, (((1,), (1,)), ((), ())), precision=HI, preferred_element_type=f32)


def mm(a, b):
    return lax.dot_general(a, b, (((1,), (0,)), ((), ())), preferred_element_type=f32)


def mmt(a, b):
    return lax.dot_general(a, b, (((1,), (1,)), ((), ())), preferred_element_type=f32)


def split(x):
    hi = x.astype(bf16)
    return hi, (x - hi.astype(f32)).astype(bf16)


def iota(shape, dim):
    return lax.broadcasted_iota(jnp.int32, shape, dim)


def left3(m):
    hi, lo = split(m)
    return jnp.concatenate([hi, lo, hi], axis=1)


def rows3(x):
    hi, lo = split(x)
    return jnp.concatenate([hi, hi, lo], axis=0)


def lanes_weights(k):
    hi, lo = split(k)
    top = jnp.concatenate([hi, lo], axis=1)
    bottom = jnp.concatenate([hi, jnp.zeros_like(lo)], axis=1)
    return jnp.concatenate([top, bottom], axis=0)


def lane_transform(x, w):
    hi, lo = split(x)
    r = mm(jnp.concatenate([hi, lo], axis=1), w)
    return r[:, :128] + r[:, 128:]


def kernel(nsub, ncg, x_ref, modes_ref, face_ref, map_ref, cols_ref, cap_any, wt_any, blk_any,
           p_out, img_out, alpha_out,
           s_ref, z_ref, w_ref, p_ref, cap_ref, blk_ref, sel_ref, am_ref, kw_ref,
           ag_ref, send1_ref, a2s_ref, a2r_ref, pick_ref, spread_ref,
           hi_ref, his_ref, hj_ref, hjs_ref, cs_ref, cr_ref,
           dsem, ag_s, ag_r, a2_s, a2_r, h_s, h_r, c_s, c_r):
    n = nsub * ncg
    s = lax.axis_index("sub")
    t = lax.axis_index("cgrp")
    me = s * ncg + t

    def peer(o):
        d = lax.rem(me + o, n)
        return d, (lax.div(d, ncg), lax.rem(d, ncg))

    barrier = pltpu.get_barrier_semaphore()

    @pl.loop(1, n)
    def _(o):
        _, dev = peer(o)
        pl.semaphore_signal(barrier, inc=1, device_id=dev, device_id_type=MESH)

    wcopy = pltpu.make_async_copy(wt_any, w_ref, dsem.at[0])
    bcopy = pltpu.make_async_copy(blk_any, blk_ref, dsem.at[1])
    ccopy = pltpu.make_async_copy(cap_any, cap_ref, dsem.at[2])
    wcopy.start()
    bcopy.start()
    ccopy.start()

    lane = iota((1, 128), 1)
    low = lane < 64
    low32 = jnp.broadcast_to(low, (32, 128))
    low64 = jnp.broadcast_to(low, (64, 128))

    def swap(a):
        return pltpu.roll(a, 64, 1)

    @pl.loop(0, 8)
    def _(c):
        r = iota((128, 512), 0)
        col = iota((128, 512), 1) + c * 512
        hit = ((col >> 6) == (r & 63)) & ((col & 63) == 63 * (r >> 6))
        sel_ref[:, pl.ds(pl.multiple_of(c * 512, 512), 512)] = jnp.where(hit, 1.0, 0.0).astype(bf16)

    for q in range(T):
        s_ref[q * 64 : q * 64 + 64, :] = x_ref[:, q * 128 : q * 128 + 128]

    fm0 = face_ref[0]
    fm1 = face_ref[1]
    r64 = iota((64, 64), 0)
    c64 = iota((64, 64), 1)
    eye64 = jnp.where(r64 == c64, 1.0, 0.0)
    qm = jnp.where(c64 == 2 * (r64 & 31) + (r64 >> 5), 1.0, 0.0)
    dup = jnp.where((iota((64, 128), 1) & 63) == iota((64, 128), 0), 1.0, 0.0)
    dupt = jnp.where((iota((128, 64), 0) & 63) == iota((128, 64), 1), 1.0, 0.0)
    eye128 = jnp.where(iota((128, 128), 0) == iota((128, 128), 1), 1.0, 0.0)
    fm11 = nn(fm1, dup)
    fm0p = nt(fm0, qm)

    y0 = s_ref[pl.ds(0, 32, stride=64), :]
    y1 = s_ref[pl.ds(63, 32, stride=64), :]
    f01 = jnp.concatenate([jnp.where(low32, y0, swap(y1)), jnp.where(low32, swap(y0), y1)], axis=0)
    f23 = jnp.where(low64, s_ref[0:64, :], s_ref[31 * 64 : 32 * 64, :])
    xh, xl = split(x_ref[...])
    f45 = mmt(jnp.concatenate([xh, xl], axis=0), sel_ref[...])
    f45 = f45[:64] + f45[64:]

    mapf = (map_ref[0, 0] & 127).astype(f32)
    mapf = jnp.concatenate([mapf, jnp.zeros((2, 128), f32)], axis=0)
    mapt = nt(eye128, mapf)
    lanef = iota((128, 128), 1).astype(f32)
    rows = []
    for pair, (left, plane) in enumerate(((fm0p, f01), (fm0, f23), (fm0, f45))):
        u = nn(left, plane) * fm11
        for half in range(2):
            keep = low if half == 0 else jnp.logical_not(low)
            val = jnp.sum(jnp.where(keep, u, 0.0), axis=1, keepdims=True)
            f = 2 * pair + half
            place = mapt[:, f : f + 1] == lanef
            rows.append(jnp.sum(jnp.where(place, val, 0.0), axis=0, keepdims=True))
    mine = jnp.concatenate(rows + [jnp.zeros((2, 128), f32)], axis=0)
    send1_ref[...] = mine
    ag_ref[me] = mine

    pl.semaphore_wait(barrier, n - 1)

    @pl.loop(1, n)
    def _(o):
        _, dev = peer(o)
        pltpu.make_async_remote_copy(src_ref=send1_ref, dst_ref=ag_ref.at[me], send_sem=ag_s, recv_sem=ag_r,
                                     device_id=dev, device_id_type=MESH).start()

    m0, m1, m2 = modes_ref[0], modes_ref[1], modes_ref[2]
    am_ref[0] = left3(m0)
    am_ref[1] = left3(nt(eye64, m0))
    am_ref[2] = left3(nt(nn(qm, m1), qm))
    am_ref[3] = left3(nt(nt(qm, m1), qm))
    block = (iota((128, 128), 0) >> 6) == (iota((128, 128), 1) >> 6)
    kw_ref[0] = lanes_weights(jnp.where(block, nn(nt(dupt, m2), dup), 0.0))
    kw_ref[1] = lanes_weights(jnp.where(block, nn(dupt, nn(m2, dup)), 0.0))

    @pl.loop(0, T // CH)
    def _(c):
        base = pl.multiple_of(c * (CH * 128), CH * 128)
        y = mm(am_ref[0], rows3(x_ref[:, pl.ds(base, CH * 128)]))
        stacked = jnp.concatenate([y[:, g * 128 : g * 128 + 128] for g in range(CH)], axis=0)
        s_ref[pl.ds(pl.multiple_of(c * (CH * 64), CH * 64), CH * 64), :] = lane_transform(stacked, kw_ref[0])

    wcopy.wait()
    for q in range(T):
        z_ref[q * 64 : q * 64 + 64, :] = w_ref[:, q * 128 : q * 128 + 128]

    def turned(ref, u):
        a = ref[pl.ds(u, 32, stride=64), :]
        b = ref[pl.ds(u + 32, 32, stride=64), :]
        return jnp.concatenate([jnp.where(low32, a, swap(b)), jnp.where(low32, swap(a), b)], axis=0)

    def middle(c, acc):
        fwd = jnp.concatenate([turned(s_ref, c * CH + g) for g in range(CH)], axis=1)
        wts = jnp.concatenate([turned(z_ref, c * CH + g) for g in range(CH)], axis=1)
        v = mm(am_ref[2], rows3(fwd))
        wv = wts * v
        prod = wv * v
        for g in range(CH):
            acc = acc + prod[:, g * 128 : g * 128 + 128]
        y = mm(am_ref[3], rows3(wv))
        for g in range(CH):
            p_ref[pl.ds(pl.multiple_of(64 + (c * CH + g) * 64, 64), 64), :] = y[:, g * 128 : g * 128 + 128]
        return acc

    gacc = lax.fori_loop(0, T // CH, middle, jnp.zeros((64, 128), f32))

    cols = cols_ref[...]
    nrow = cols.shape[0]
    nz = cols.shape[1]
    wide_cols = jnp.concatenate([jnp.broadcast_to(cols[i : i + 1, :], (nz, nz)) for i in range(nrow)], axis=0)
    kk = nrow * nz
    pick_diag = iota((kk, nz), 1) == (iota((kk, nz), 0) & (nz - 1))
    colv = jnp.sum(jnp.where(pick_diag, wide_cols.astype(f32), 0.0), axis=1, keepdims=True)
    r = iota((1, n * 8), 1)
    d = r >> 3
    f = r & 7
    own = nrow * d + f
    own = jnp.where((f == 0) & (d >= ncg), nrow * (d - ncg) + 1, own)
    own = jnp.where((f == 2) & (lax.rem(d, ncg) > 0), nrow * (d - 1) + 3, own)
    own = jnp.where(f >= 6, -1, own).astype(f32)
    g1 = jnp.where(colv == own, 1.0, 0.0)
    g1 = jnp.concatenate([g1, jnp.zeros((128 - kk, n * 8), f32)], axis=0)

    pltpu.make_async_copy(ag_ref.at[pl.ds(0, n - 1)], ag_ref.at[pl.ds(0, n - 1)], ag_r).wait()
    picked = nn(g1, ag_ref[...].reshape(n * 8, 128))
    pick_ref[...] = picked[:kk].reshape(nrow, nz, 128)
    bcopy.wait()
    spread_ref[...] = jnp.zeros_like(spread_ref)

    def coarse_row(i, acc):
        pk = pick_ref[i]
        tot = blk_ref[i, 0] * pk[0:1]
        for k in range(1, nz):
            tot = tot + blk_ref[i, k] * pk[k : k + 1]
        img = jnp.sum(tot, axis=1, keepdims=True)
        out = [jnp.sum(blk_ref[i, k] * img, axis=0, keepdims=True) for k in range(nz)]
        spread_ref[i] = jnp.concatenate(out, axis=0)
        return acc + img * img

    iacc = lax.fori_loop(0, nrow, coarse_row, jnp.zeros((128, 1), f32))
    gpart = jnp.sum(iacc, keepdims=True) + jnp.sum(gacc, keepdims=True)
    back = nn(g1.T, spread_ref[...].reshape(128, 128))
    back = jnp.where((iota((n * 8, 128), 0) & 7) == 6, gpart, back)
    a2s_ref[...] = back.reshape(n, 8, 128)
    a2r_ref[me] = a2s_ref[me]

    @pl.loop(1, n)
    def _(o):
        dd, dev = peer(o)
        pltpu.make_async_remote_copy(src_ref=a2s_ref.at[dd], dst_ref=a2r_ref.at[me], send_sem=a2_s, recv_sem=a2_r,
                                     device_id=dev, device_id_type=MESH).start()

    @pl.loop(0, T // CH)
    def _(c):
        tiles = []
        for g in range(CH):
            a = p_ref[pl.ds(64 + c * CH + g, 32, stride=64), :]
            b = p_ref[pl.ds(96 + c * CH + g, 32, stride=64), :]
            tiles.append(jnp.where(low32, a, swap(b)))
            tiles.append(jnp.where(low32, swap(a), b))
        k = lane_transform(jnp.concatenate(tiles, axis=0), kw_ref[1])
        y = jnp.concatenate([k[g * 64 : g * 64 + 64] for g in range(CH)], axis=1)
        y = mm(am_ref[1], rows3(y))
        for g in range(CH):
            s_ref[pl.ds(pl.multiple_of((c * CH + g) * 64, 64), 64), :] = y[:, g * 128 : g * 128 + 128]

    fm0t = nt(eye64, fm0)
    fm0pt = nt(qm, fm0)

    pltpu.make_async_copy(a2r_ref.at[pl.ds(0, n - 1)], a2r_ref.at[pl.ds(0, n - 1)], a2_r).wait()
    backs = jnp.sum(a2r_ref[...], axis=0)
    gamma = backs[6:7, :]
    corr = []
    for f in range(6):
        place = mapt[:, f : f + 1] == lanef
        corr.append(jnp.sum(jnp.where(place, backs[f : f + 1], 0.0), axis=1, keepdims=True))
    e01 = nn(fm0pt, jnp.where(low, corr[0], corr[1]) * fm11)
    e23 = nn(fm0t, jnp.where(low, corr[2], corr[3]) * fm11)
    e45 = nn(fm0t, jnp.where(low, corr[4], corr[5]) * fm11)
    eh, el = split(e45)
    eh = jnp.concatenate([eh, el], axis=0)

    @pl.loop(0, T // CH)
    def _(c):
        base = pl.multiple_of(c * (CH * 128), CH * 128)
        add = mm(eh, sel_ref[:, pl.ds(base, CH * 128)])
        for g in range(CH):
            at = pl.multiple_of((c * CH + g) * 64, 64)
            tile = add[:64, g * 128 : g * 128 + 128] + add[64:, g * 128 : g * 128 + 128]
            p_ref[pl.ds(at + 64, 64), :] = s_ref[pl.ds(at, 64), :] + tile

    p_ref[64:128, :] += jnp.where(low64, e23, 0.0)
    p_ref[T * 64 : T * 64 + 64, :] += jnp.where(low64, 0.0, e23)
    top, bottom = e01[:32], e01[32:]
    edge0 = p_ref[pl.ds(64, 32, stride=64), :] + jnp.where(low32, top, swap(bottom))
    edge1 = p_ref[pl.ds(64 + 63, 32, stride=64), :] + jnp.where(low32, swap(top), bottom)
    p_ref[pl.ds(64, 32, stride=64), :] = edge0
    p_ref[pl.ds(64 + 63, 32, stride=64), :] = edge1

    his_ref[0] = edge0
    his_ref[1] = edge1
    hjs_ref[0] = p_ref[64:128, :]
    hjs_ref[1] = p_ref[T * 64 : T * 64 + 64, :]

    sends = (
        (s > 0, s < nsub - 1, (s - 1, t), his_ref, hi_ref, 0, 1, 0),
        (s < nsub - 1, s > 0, (s + 1, t), his_ref, hi_ref, 1, 0, 1),
        (t > 0, t < ncg - 1, (s, t - 1), hjs_ref, hj_ref, 0, 1, 2),
        (t < ncg - 1, t > 0, (s, t + 1), hjs_ref, hj_ref, 1, 0, 3),
    )

    def halo(dev, src, dst, a, b, k):
        return pltpu.make_async_remote_copy(src_ref=src.at[a], dst_ref=dst.at[b], send_sem=h_s.at[k],
                                            recv_sem=h_r.at[k], device_id=dev, device_id_type=MESH)

    for does, gets, dev, src, dst, a, b, k in sends:
        @pl.when(does)
        def _():
            halo(dev, src, dst, a, b, k).start()

        @pl.when(jnp.logical_not(gets))
        def _():
            dst[b] = jnp.zeros(dst.shape[1:], f32)

    ccopy.wait()
    for does, gets, dev, src, dst, a, b, k in sends:
        @pl.when(gets)
        def _():
            halo(dev, src, dst, a, b, k).wait_recv()

    p_ref[0:64, :] = hj_ref[0]
    p_ref[(T + 1) * 64 : (T + 2) * 64, :] = hj_ref[1]

    row = iota((64, 128), 0)
    kpos = iota((64, 128), 1) & 63

    def stencil(q, acc):
        at = pl.multiple_of(q * 64, 64)
        x = p_ref[pl.ds(at + 64, 64), :]
        here = swap(x)
        before = swap(p_ref[pl.ds(at, 64), :])
        after = swap(p_ref[pl.ds(at + 128, 64), :])
        second = here + jnp.where(low64, before, after)
        up = jnp.where(row == 0, hi_ref[0, pl.ds(q, 1), :], pltpu.roll(x, 1, 0))
        down = jnp.where(row == 63, hi_ref[1, pl.ds(q, 1), :], pltpu.roll(x, 63, 0))
        third = jnp.where(kpos == 0, 0.0, pltpu.roll(x, 1, 1)) + jnp.where(kpos == 63, 0.0, pltpu.roll(x, 127, 1))
        cols_at = pl.ds(pl.multiple_of(q * 128, 128), 128)
        img = (cap_ref[:, cols_at] + 8.2) * x - (up + down) - 0.6 * second - 2.5 * third
        img_out[:, cols_at] = img
        p_out[:, cols_at] = x
        return acc + x * img

    cacc = lax.fori_loop(0, T, stencil, jnp.zeros((64, 128), f32))
    cpart = jnp.sum(cacc, axis=0, keepdims=True)
    cs_ref[...] = cpart
    cr_ref[me] = cpart

    @pl.loop(1, n)
    def _(o):
        _, dev = peer(o)
        pltpu.make_async_remote_copy(src_ref=cs_ref, dst_ref=cr_ref.at[me], send_sem=c_s, recv_sem=c_r,
                                     device_id=dev, device_id_type=MESH).start()

    pltpu.make_async_copy(cr_ref.at[pl.ds(0, n - 1)], cr_ref.at[pl.ds(0, n - 1)], c_r).wait()
    curv = jnp.sum(jnp.sum(cr_ref[...], axis=0), axis=1, keepdims=True)
    alpha_out[...] = jnp.broadcast_to(gamma / curv, (8, 128))

    pltpu.make_async_copy(ag_ref.at[pl.ds(0, n - 1)], ag_ref.at[pl.ds(0, n - 1)], ag_s).wait()
    pltpu.make_async_copy(a2r_ref.at[pl.ds(0, n - 1)], a2r_ref.at[pl.ds(0, n - 1)], a2_s).wait()
    pltpu.make_async_copy(cr_ref.at[pl.ds(0, n - 1)], cr_ref.at[pl.ds(0, n - 1)], c_s).wait()
    for does, gets, dev, src, dst, a, b, k in sends:
        @pl.when(does)
        def _():
            halo(dev, src, dst, a, b, k).wait_send()


def body(nsub, ncg, source, capacity, fd_weights, fd_modes, face_modes, coarse_map, fsai_cols, fsai_blocks):
    n = nsub * ncg
    nrow, nz = fsai_cols.shape
    vm = pl.BlockSpec(memory_space=pltpu.VMEM)
    hbm = pl.BlockSpec(memory_space=pl.ANY)
    field = jax.ShapeDtypeStruct(source.shape, f32)
    V = pltpu.VMEM
    dma = pltpu.SemaphoreType.DMA
    p, img, alpha = pl.pallas_call(
        functools.partial(kernel, nsub, ncg),
        out_shape=(field, field, jax.ShapeDtypeStruct((8, 128), f32)),
        in_specs=[vm] * 5 + [hbm] * 3,
        out_specs=(vm, vm, vm),
        scratch_shapes=[
            V((T * 64, 128), f32),
            V((T * 64, 128), f32),
            V((64, T * 128), f32),
            V(((T + 2) * 64, 128), f32),
            V((64, T * 128), f32),
            V(fsai_blocks.shape, f32),
            V((128, T * 128), bf16),
            V((4, 64, 192), bf16),
            V((2, 256, 256), bf16),
            V((n, 8, 128), f32),
            V((8, 128), f32),
            V((n, 8, 128), f32),
            V((n, 8, 128), f32),
            V((nrow, nz, 128), f32),
            V((128 // nz, nz, 128), f32),
            V((2, 32, 128), f32),
            V((2, 32, 128), f32),
            V((2, 64, 128), f32),
            V((2, 64, 128), f32),
            V((1, 128), f32),
            V((n, 1, 128), f32),
            dma((3,)),
            dma, dma, dma, dma,
            dma((4,)), dma((4,)),
            dma, dma,
        ],
        compiler_params=pltpu.CompilerParams(collective_id=0, has_side_effects=True,
                                             vmem_limit_bytes=48 * 1024 * 1024),
        cost_estimate=pl.CostEstimate(flops=10**9, bytes_accessed=8 * 2**20, transcendentals=0),
        name="step",
    )(source, fd_modes, face_modes, coarse_map, fsai_cols, capacity, fd_weights, fsai_blocks)
    a = alpha[0, 0]
    return a * p, source - a * img


def solution(mesh):
    in_specs = (
        P("sub", "cgrp"),
        P("sub", "cgrp"),
        P("sub", "cgrp"),
        P(),
        P(),
        P("sub", "cgrp", None, None),
        P(("sub", "cgrp"), None),
        P(("sub", "cgrp"), None, None, None),
    )
    out_specs = (P("sub", "cgrp"), P("sub", "cgrp"))
    step = functools.partial(body, mesh.shape["sub"], mesh.shape["cgrp"])
    return jax.shard_map(step, mesh=mesh, in_specs=in_specs, out_specs=out_specs, check_vma=False)
```

```python
import functools
import jax
import jax.numpy as jnp
from jax import lax
from jax.experimental import pallas as pl
from jax.experimental.pallas import tpu as pltpu
from jax.sharding import PartitionSpec as P

C = 64
T = 32
CH = 8
f32 = jnp.float32
bf16 = jnp.bfloat16
HI = lax.Precision.HIGHEST
MESH = pl.DeviceIdType.MESH


def nn(a, b):
    return lax.dot_general(a, b, (((1,), (0,)), ((), ())), precision=HI, preferred_element_type=f32)


def nt(a, b):
    return lax.dot_general(a, b, (((1,), (1,)), ((), ())), precision=HI, preferred_element_type=f32)


def mm(a, b):
    return lax.dot_general(a, b, (((1,), (0,)), ((), ())), preferred_element_type=f32)


def mmt(a, b):
    return lax.dot_general(a, b, (((1,), (1,)), ((), ())), preferred_element_type=f32)


def split(x):
    hi = x.astype(bf16)
    return hi, (x - hi.astype(f32)).astype(bf16)


def iota(shape, dim):
    return lax.broadcasted_iota(jnp.int32, shape, dim)


def left3(m):
    hi, lo = split(m)
    return jnp.concatenate([hi, lo, hi], axis=1)


def rows3(x):
    hi, lo = split(x)
    return jnp.concatenate([hi, hi, lo], axis=0)


def lanes_weights(k):
    hi, lo = split(k)
    top = jnp.concatenate([hi, lo], axis=1)
    bottom = jnp.concatenate([hi, jnp.zeros_like(lo)], axis=1)
    return jnp.concatenate([top, bottom], axis=0)


def lane_transform(x, w):
    hi, lo = split(x)
    r = mm(jnp.concatenate([hi, lo], axis=1), w)
    return r[:, :128] + r[:, 128:]


def kernel(nsub, ncg, x_any, modes_any, face_any, map_any, cols_any, cap_any, wt_any, blk_any,
           p_out, img_out, alpha_out,
           x_ref, modes_ref, face_ref, map_ref, cols_ref,
           s_ref, z_ref, w_ref, p_ref, cap_ref, blk_ref, sel_ref, am_ref, kw_ref,
           ag_ref, send1_ref, a2s_ref, a2r_ref, pick_ref, spread_ref,
           hi_ref, his_ref, hj_ref, hjs_ref, cs_ref, cr_ref,
           dsem, ag_s, ag_r, a2_s, a2_r, h_s, h_r, c_s, c_r, osem):
    n = nsub * ncg
    s = lax.axis_index("sub")
    t = lax.axis_index("cgrp")
    me = s * ncg + t

    def peer(o):
        d = lax.rem(me + o, n)
        return d, (lax.div(d, ncg), lax.rem(d, ncg))

    early = []
    for k, (src, dst) in enumerate(((face_any, face_ref), (map_any, map_ref), (x_any, x_ref),
                                    (modes_any, modes_ref), (cols_any, cols_ref),
                                    (wt_any, w_ref), (blk_any, blk_ref), (cap_any, cap_ref))):
        early.append(pltpu.make_async_copy(src, dst, dsem.at[k]))
        early[-1].start()
    fcopy, mcopy, xcopy, ocopy, lcopy, wcopy, bcopy, ccopy = early

    barrier = pltpu.get_barrier_semaphore()

    @pl.loop(1, n)
    def _(o):
        _, dev = peer(o)
        pl.semaphore_signal(barrier, inc=1, device_id=dev, device_id_type=MESH)

    lane = iota((1, 128), 1)
    low = lane < 64
    low32 = jnp.broadcast_to(low, (32, 128))
    low64 = jnp.broadcast_to(low, (64, 128))

    def swap(a):
        return pltpu.roll(a, 64, 1)

    @pl.loop(0, 8)
    def _(c):
        r = iota((128, 512), 0)
        col = iota((128, 512), 1) + c * 512
        hit = ((col >> 6) == (r & 63)) & ((col & 63) == 63 * (r >> 6))
        sel_ref[:, pl.ds(pl.multiple_of(c * 512, 512), 512)] = jnp.where(hit, 1.0, 0.0).astype(bf16)

    fcopy.wait()
    mcopy.wait()
    fm0t = face_ref[0]
    fm1t = face_ref[1]
    r64 = iota((64, 64), 0)
    c64 = iota((64, 64), 1)
    eye64 = jnp.where(r64 == c64, 1.0, 0.0)
    qm = jnp.where(c64 == 2 * (r64 & 31) + (r64 >> 5), 1.0, 0.0)
    dup = jnp.where((iota((64, 128), 1) & 63) == iota((64, 128), 0), 1.0, 0.0)
    dupt = jnp.where((iota((128, 64), 0) & 63) == iota((128, 64), 1), 1.0, 0.0)
    eye128 = jnp.where(iota((128, 128), 0) == iota((128, 128), 1), 1.0, 0.0)
    fm0pt = nn(qm, fm0t)
    fm0 = nt(eye128, fm0t)
    fm0p = nt(eye128, fm0pt)
    fm11 = nt(eye128, jnp.concatenate([fm1t, fm1t], axis=0))

    mapf = [(map_ref[f] & 127).astype(f32) for f in range(6)]
    mapf = jnp.concatenate(mapf + [jnp.zeros((2, 128), f32)], axis=0)
    mapt = nt(eye128, mapf)
    lanef = iota((128, 128), 1).astype(f32)

    xcopy.wait()
    for q in range(T):
        s_ref[q * 8 : q * 8 + 8, :] = x_ref[0:8, q * 128 : q * 128 + 128]
        s_ref[256 + q * 8 : 256 + q * 8 + 8, :] = x_ref[56:64, q * 128 : q * 128 + 128]
    y0 = s_ref[pl.ds(0, 32, stride=8), :]
    y1 = s_ref[pl.ds(263, 32, stride=8), :]
    f01 = jnp.concatenate([jnp.where(low32, y0, swap(y1)), jnp.where(low32, swap(y0), y1)], axis=0)
    f23 = jnp.where(low64, x_ref[:, :128], x_ref[:, 31 * 128 :])
    xh, xl = split(x_ref[...])
    f45 = mmt(jnp.concatenate([xh, xl], axis=0), sel_ref[...])
    f45 = f45[:64] + f45[64:]

    rows = []
    for pair, (left, plane) in enumerate(((fm0p, f01), (fm0, f23), (fm0, f45))):
        u = mm(left3(left), rows3(plane)) * fm11
        for half in range(2):
            keep = low if half == 0 else jnp.logical_not(low)
            val = jnp.sum(jnp.where(keep, u, 0.0), axis=1, keepdims=True)
            f = 2 * pair + half
            place = mapt[:, f : f + 1] == lanef
            rows.append(jnp.sum(jnp.where(place, val, 0.0), axis=0, keepdims=True))
    mine = jnp.concatenate(rows + [jnp.zeros((2, 128), f32)], axis=0)
    send1_ref[...] = mine
    ag_ref[me] = mine

    pl.semaphore_wait(barrier, n - 1)

    @pl.loop(1, n)
    def _(o):
        _, dev = peer(o)
        pltpu.make_async_remote_copy(src_ref=send1_ref, dst_ref=ag_ref.at[me], send_sem=ag_s, recv_sem=ag_r,
                                     device_id=dev, device_id_type=MESH).start()

    ocopy.wait()
    m0, m1, m2 = modes_ref[0], modes_ref[1], modes_ref[2]
    am_ref[0] = left3(m0)
    am_ref[1] = left3(nt(eye64, m0))
    am_ref[2] = left3(nt(nn(qm, m1), qm))
    am_ref[3] = left3(nt(nt(qm, m1), qm))
    block = (iota((128, 128), 0) >> 6) == (iota((128, 128), 1) >> 6)
    kw_ref[0] = lanes_weights(jnp.where(block, nn(nt(dupt, m2), dup), 0.0))
    kw_ref[1] = lanes_weights(jnp.where(block, nn(dupt, nn(m2, dup)), 0.0))

    @pl.loop(0, T // CH)
    def _(c):
        base = pl.multiple_of(c * (CH * 128), CH * 128)
        y = mm(am_ref[0], rows3(x_ref[:, pl.ds(base, CH * 128)]))
        stacked = jnp.concatenate([y[:, g * 128 : g * 128 + 128] for g in range(CH)], axis=0)
        s_ref[pl.ds(pl.multiple_of(c * (CH * 64), CH * 64), CH * 64), :] = lane_transform(stacked, kw_ref[0])

    wcopy.wait()
    for q in range(T):
        z_ref[q * 64 : q * 64 + 64, :] = w_ref[:, q * 128 : q * 128 + 128]

    def turned(ref, u):
        a = ref[pl.ds(u, 32, stride=64), :]
        b = ref[pl.ds(u + 32, 32, stride=64), :]
        return jnp.concatenate([jnp.where(low32, a, swap(b)), jnp.where(low32, swap(a), b)], axis=0)

    def middle(c, acc):
        fwd = jnp.concatenate([turned(s_ref, c * CH + g) for g in range(CH)], axis=1)
        wts = jnp.concatenate([turned(z_ref, c * CH + g) for g in range(CH)], axis=1)
        v = mm(am_ref[2], rows3(fwd))
        wv = wts * v
        prod = wv * v
        for g in range(CH):
            acc = acc + prod[:, g * 128 : g * 128 + 128]
        y = mm(am_ref[3], rows3(wv))
        for g in range(CH):
            p_ref[pl.ds(pl.multiple_of(64 + (c * CH + g) * 64, 64), 64), :] = y[:, g * 128 : g * 128 + 128]
        return acc

    gacc = lax.fori_loop(0, T // CH, middle, jnp.zeros((64, 128), f32))

    lcopy.wait()
    cols = cols_ref[...]
    nrow = cols.shape[0]
    nz = cols.shape[1]
    wide_cols = jnp.concatenate([jnp.broadcast_to(cols[i : i + 1, :], (nz, nz)) for i in range(nrow)], axis=0)
    kk = nrow * nz
    pick_diag = iota((kk, nz), 1) == (iota((kk, nz), 0) & (nz - 1))
    colv = jnp.sum(jnp.where(pick_diag, wide_cols.astype(f32), 0.0), axis=1, keepdims=True)
    r = iota((1, n * 8), 1)
    d = r >> 3
    f = r & 7
    own = nrow * d + f
    own = jnp.where((f == 0) & (d >= ncg), nrow * (d - ncg) + 1, own)
    own = jnp.where((f == 2) & (lax.rem(d, ncg) > 0), nrow * (d - 1) + 3, own)
    own = jnp.where(f >= 6, -1, own).astype(f32)
    g1 = jnp.where(colv == own, 1.0, 0.0)
    g1 = jnp.concatenate([g1, jnp.zeros((128 - kk, n * 8), f32)], axis=0)

    pltpu.make_async_copy(ag_ref.at[pl.ds(0, n - 1)], ag_ref.at[pl.ds(0, n - 1)], ag_r).wait()
    picked = nn(g1, ag_ref[...].reshape(n * 8, 128))
    pick_ref[...] = picked[:kk].reshape(nrow, nz, 128)
    bcopy.wait()
    spread_ref[...] = jnp.zeros_like(spread_ref)

    def coarse_row(i, acc):
        pk = pick_ref[i]
        tot = blk_ref[i, 0] * pk[0:1]
        for k in range(1, nz):
            tot = tot + blk_ref[i, k] * pk[k : k + 1]
        img = jnp.sum(tot, axis=1, keepdims=True)
        out = [jnp.sum(blk_ref[i, k] * img, axis=0, keepdims=True) for k in range(nz)]
        spread_ref[i] = jnp.concatenate(out, axis=0)
        return acc + img * img

    iacc = lax.fori_loop(0, nrow, coarse_row, jnp.zeros((128, 1), f32))
    gpart = jnp.sum(iacc, keepdims=True) + jnp.sum(gacc, keepdims=True)
    back = nn(g1.T, spread_ref[...].reshape(128, 128))
    back = jnp.where((iota((n * 8, 128), 0) & 7) == 6, gpart, back)
    a2s_ref[...] = back.reshape(n, 8, 128)
    a2r_ref[me] = a2s_ref[me]

    @pl.loop(1, n)
    def _(o):
        dd, dev = peer(o)
        pltpu.make_async_remote_copy(src_ref=a2s_ref.at[dd], dst_ref=a2r_ref.at[me], send_sem=a2_s, recv_sem=a2_r,
                                     device_id=dev, device_id_type=MESH).start()

    @pl.loop(0, T // CH)
    def _(c):
        tiles = []
        for g in range(CH):
            a = p_ref[pl.ds(64 + c * CH + g, 32, stride=64), :]
            b = p_ref[pl.ds(96 + c * CH + g, 32, stride=64), :]
            tiles.append(jnp.where(low32, a, swap(b)))
            tiles.append(jnp.where(low32, swap(a), b))
        k = lane_transform(jnp.concatenate(tiles, axis=0), kw_ref[1])
        y = jnp.concatenate([k[g * 64 : g * 64 + 64] for g in range(CH)], axis=1)
        y = mm(am_ref[1], rows3(y))
        for g in range(CH):
            s_ref[pl.ds(pl.multiple_of((c * CH + g) * 64, 64), 64), :] = y[:, g * 128 : g * 128 + 128]

    pltpu.make_async_copy(a2r_ref.at[pl.ds(0, n - 1)], a2r_ref.at[pl.ds(0, n - 1)], a2_r).wait()
    backs = jnp.sum(a2r_ref[...], axis=0)
    gamma = backs[6:7, :]
    corr = []
    for f in range(6):
        place = mapt[:, f : f + 1] == lanef
        corr.append(jnp.sum(jnp.where(place, backs[f : f + 1], 0.0), axis=1, keepdims=True))
    e01 = mm(left3(fm0pt), rows3(jnp.where(low, corr[0], corr[1]) * fm11))
    e23 = mm(left3(fm0t), rows3(jnp.where(low, corr[2], corr[3]) * fm11))
    e45 = mm(left3(fm0t), rows3(jnp.where(low, corr[4], corr[5]) * fm11))
    eh, el = split(e45)
    eh = jnp.concatenate([eh, el], axis=0)

    @pl.loop(0, T // CH)
    def _(c):
        base = pl.multiple_of(c * (CH * 128), CH * 128)
        add = mm(eh, sel_ref[:, pl.ds(base, CH * 128)])
        for g in range(CH):
            at = pl.multiple_of((c * CH + g) * 64, 64)
            tile = add[:64, g * 128 : g * 128 + 128] + add[64:, g * 128 : g * 128 + 128]
            p_ref[pl.ds(at + 64, 64), :] = s_ref[pl.ds(at, 64), :] + tile

    p_ref[64:128, :] += jnp.where(low64, e23, 0.0)
    p_ref[T * 64 : T * 64 + 64, :] += jnp.where(low64, 0.0, e23)
    top, bottom = e01[:32], e01[32:]
    edge0 = p_ref[pl.ds(64, 32, stride=64), :] + jnp.where(low32, top, swap(bottom))
    edge1 = p_ref[pl.ds(64 + 63, 32, stride=64), :] + jnp.where(low32, swap(top), bottom)
    p_ref[pl.ds(64, 32, stride=64), :] = edge0
    p_ref[pl.ds(64 + 63, 32, stride=64), :] = edge1

    his_ref[0] = edge0
    his_ref[1] = edge1
    hjs_ref[0] = p_ref[64:128, :]
    hjs_ref[1] = p_ref[T * 64 : T * 64 + 64, :]

    sends = (
        (s > 0, s < nsub - 1, (s - 1, t), his_ref, hi_ref, 0, 1, 0),
        (s < nsub - 1, s > 0, (s + 1, t), his_ref, hi_ref, 1, 0, 1),
        (t > 0, t < ncg - 1, (s, t - 1), hjs_ref, hj_ref, 0, 1, 2),
        (t < ncg - 1, t > 0, (s, t + 1), hjs_ref, hj_ref, 1, 0, 3),
    )

    def halo(dev, src, dst, a, b, k):
        return pltpu.make_async_remote_copy(src_ref=src.at[a], dst_ref=dst.at[b], send_sem=h_s.at[k],
                                            recv_sem=h_r.at[k], device_id=dev, device_id_type=MESH)

    for does, gets, dev, src, dst, a, b, k in sends:
        @pl.when(does)
        def _():
            halo(dev, src, dst, a, b, k).start()

        @pl.when(jnp.logical_not(gets))
        def _():
            dst[b] = jnp.zeros(dst.shape[1:], f32)

    ccopy.wait()
    for does, gets, dev, src, dst, a, b, k in sends:
        @pl.when(gets)
        def _():
            halo(dev, src, dst, a, b, k).wait_recv()

    p_ref[0:64, :] = hj_ref[0]
    p_ref[(T + 1) * 64 : (T + 2) * 64, :] = hj_ref[1]

    row = iota((64, 128), 0)
    kpos = iota((64, 128), 1) & 63

    def stencil(q, acc):
        at = pl.multiple_of(q * 64, 64)
        x = p_ref[pl.ds(at + 64, 64), :]
        here = swap(x)
        before = swap(p_ref[pl.ds(at, 64), :])
        after = swap(p_ref[pl.ds(at + 128, 64), :])
        second = here + jnp.where(low64, before, after)
        up = jnp.where(row == 0, hi_ref[0, pl.ds(q, 1), :], pltpu.roll(x, 1, 0))
        down = jnp.where(row == 63, hi_ref[1, pl.ds(q, 1), :], pltpu.roll(x, 63, 0))
        third = jnp.where(kpos == 0, 0.0, pltpu.roll(x, 1, 1)) + jnp.where(kpos == 63, 0.0, pltpu.roll(x, 127, 1))
        cols_at = pl.ds(pl.multiple_of(q * 128, 128), 128)
        img = (cap_ref[:, cols_at] + 8.2) * x - (up + down) - 0.6 * second - 2.5 * third
        z_ref[pl.ds(at, 64), :] = img
        pltpu.make_async_copy(p_ref.at[pl.ds(at + 64, 64), :], p_out.at[:, cols_at], osem.at[0]).start()
        pltpu.make_async_copy(z_ref.at[pl.ds(at, 64), :], img_out.at[:, cols_at], osem.at[1]).start()
        return acc + x * img

    cacc = lax.fori_loop(0, T, stencil, jnp.zeros((64, 128), f32))
    cpart = jnp.sum(cacc, axis=0, keepdims=True)
    cs_ref[...] = cpart
    cr_ref[me] = cpart

    @pl.loop(1, n)
    def _(o):
        _, dev = peer(o)
        pltpu.make_async_remote_copy(src_ref=cs_ref, dst_ref=cr_ref.at[me], send_sem=c_s, recv_sem=c_r,
                                     device_id=dev, device_id_type=MESH).start()

    pltpu.make_async_copy(cr_ref.at[pl.ds(0, n - 1)], cr_ref.at[pl.ds(0, n - 1)], c_r).wait()
    curv = jnp.sum(jnp.sum(cr_ref[...], axis=0), axis=1, keepdims=True)
    alpha_out[...] = gamma[:, 0:1] / curv

    pltpu.make_async_copy(z_ref, z_ref, osem.at[0]).wait()
    pltpu.make_async_copy(z_ref, z_ref, osem.at[1]).wait()
    pltpu.make_async_copy(ag_ref.at[pl.ds(0, n - 1)], ag_ref.at[pl.ds(0, n - 1)], ag_s).wait()
    pltpu.make_async_copy(a2r_ref.at[pl.ds(0, n - 1)], a2r_ref.at[pl.ds(0, n - 1)], a2_s).wait()
    pltpu.make_async_copy(cr_ref.at[pl.ds(0, n - 1)], cr_ref.at[pl.ds(0, n - 1)], c_s).wait()
    for does, gets, dev, src, dst, a, b, k in sends:
        @pl.when(does)
        def _():
            halo(dev, src, dst, a, b, k).wait_send()


def body(nsub, ncg, source, capacity, fd_weights, fd_modes, face_modes, coarse_map, fsai_cols, fsai_blocks):
    n = nsub * ncg
    nrow, nz = fsai_cols.shape
    vm = pl.BlockSpec(memory_space=pltpu.VMEM)
    hbm = pl.BlockSpec(memory_space=pltpu.HBM)
    field = jax.ShapeDtypeStruct(source.shape, f32)
    V = pltpu.VMEM
    dma = pltpu.SemaphoreType.DMA
    p, img, alpha = pl.pallas_call(
        functools.partial(kernel, nsub, ncg),
        out_shape=(field, field, jax.ShapeDtypeStruct((1, 1), f32)),
        in_specs=[hbm] * 8,
        out_specs=(hbm, hbm, vm),
        scratch_shapes=[
            V(source.shape, f32),
            V(fd_modes.shape, f32),
            V((2, 64, 128), f32),
            V((6, 1, 128), jnp.int32),
            V(fsai_cols.shape, jnp.int32),
            V((T * 64, 128), f32),
            V((T * 64, 128), f32),
            V((64, T * 128), f32),
            V(((T + 2) * 64, 128), f32),
            V((64, T * 128), f32),
            V(fsai_blocks.shape, f32),
            V((128, T * 128), bf16),
            V((4, 64, 192), bf16),
            V((2, 256, 256), bf16),
            V((n, 8, 128), f32),
            V((8, 128), f32),
            V((n, 8, 128), f32),
            V((n, 8, 128), f32),
            V((nrow, nz, 128), f32),
            V((128 // nz, nz, 128), f32),
            V((2, 32, 128), f32),
            V((2, 32, 128), f32),
            V((2, 64, 128), f32),
            V((2, 64, 128), f32),
            V((1, 128), f32),
            V((n, 1, 128), f32),
            dma((8,)),
            dma, dma, dma, dma,
            dma((4,)), dma((4,)),
            dma, dma,
            dma((2,)),
        ],
        compiler_params=pltpu.CompilerParams(collective_id=0, has_side_effects=True,
                                             vmem_limit_bytes=60 * 1024 * 1024),
        cost_estimate=pl.CostEstimate(flops=10**9, bytes_accessed=8 * 2**20, transcendentals=0),
        name="step",
    )(source, fd_modes, jnp.swapaxes(face_modes, 1, 2), coarse_map.reshape(-1, 1, coarse_map.shape[-1]),
      fsai_cols, capacity, fd_weights, fsai_blocks)
    a = alpha[0, 0]
    return a * p, source - a * img


def solution(mesh):
    in_specs = (
        P("sub", "cgrp"),
        P("sub", "cgrp"),
        P("sub", "cgrp"),
        P(),
        P(),
        P("sub", "cgrp", None, None),
        P(("sub", "cgrp"), None),
        P(("sub", "cgrp"), None, None, None),
    )
    out_specs = (P("sub", "cgrp"), P("sub", "cgrp"))
    step = functools.partial(body, mesh.shape["sub"], mesh.shape["cgrp"])
    return jax.shard_map(step, mesh=mesh, in_specs=in_specs, out_specs=out_specs, check_vma=False)
```

```python
import functools
import jax
import jax.numpy as jnp
from jax import lax
from jax.experimental import pallas as pl
from jax.experimental.pallas import tpu as pltpu
from jax.sharding import PartitionSpec as P

C = 64
T = 32
CH = 8
f32 = jnp.float32
bf16 = jnp.bfloat16
HI = lax.Precision.HIGHEST
MESH = pl.DeviceIdType.MESH


def nn(a, b):
    return lax.dot_general(a, b, (((1,), (0,)), ((), ())), precision=HI, preferred_element_type=f32)


def nt(a, b):
    return lax.dot_general(a, b, (((1,), (1,)), ((), ())), precision=HI, preferred_element_type=f32)


def mm(a, b):
    return lax.dot_general(a, b, (((1,), (0,)), ((), ())), preferred_element_type=f32)


def mmt(a, b):
    return lax.dot_general(a, b, (((1,), (1,)), ((), ())), preferred_element_type=f32)


def split(x):
    hi = x.astype(bf16)
    return hi, (x - hi.astype(f32)).astype(bf16)


def iota(shape, dim):
    return lax.broadcasted_iota(jnp.int32, shape, dim)


def left3(m):
    hi, lo = split(m)
    return jnp.concatenate([hi, lo, hi], axis=1)


def rows3(x):
    hi, lo = split(x)
    return jnp.concatenate([hi, hi, lo], axis=0)


def lanes_weights(k):
    hi, lo = split(k)
    top = jnp.concatenate([hi, lo], axis=1)
    bottom = jnp.concatenate([hi, jnp.zeros_like(lo)], axis=1)
    return jnp.concatenate([top, bottom], axis=0)


def lane_transform(x, w):
    hi, lo = split(x)
    r = mm(jnp.concatenate([hi, lo], axis=1), w)
    return r[:, :128] + r[:, 128:]


def kernel(nsub, ncg, x_any, modes_any, face_any, map_any, cols_any, cap_any, wt_any, blk_any,
           p_out, img_out, alpha_out,
           x_ref, modes_ref, face_ref, map_ref, cols_ref,
           s_ref, z_ref, w_ref, p_ref, cap_ref, blk_ref, sel_ref, am_ref, kw_ref,
           ag_ref, send1_ref, a2s_ref, a2r_ref, pick_ref, spread_ref,
           hi_ref, his_ref, hj_ref, hjs_ref, cs_ref, cr_ref,
           dsem, ag_s, ag_r, a2_s, a2_r, h_s, h_r, c_s, c_r):
    n = nsub * ncg
    s = lax.axis_index("sub")
    t = lax.axis_index("cgrp")
    me = s * ncg + t

    def peer(o):
        d = lax.rem(me + o, n)
        return d, (lax.div(d, ncg), lax.rem(d, ncg))

    early = []
    for k, (src, dst) in enumerate(((face_any, face_ref), (map_any, map_ref), (x_any, x_ref),
                                    (modes_any, modes_ref), (cols_any, cols_ref),
                                    (wt_any, w_ref), (blk_any, blk_ref), (cap_any, cap_ref))):
        early.append(pltpu.make_async_copy(src, dst, dsem.at[k]))
        early[-1].start()
    fcopy, mcopy, xcopy, ocopy, lcopy, wcopy, bcopy, ccopy = early

    barrier = pltpu.get_barrier_semaphore()

    @pl.loop(1, n)
    def _(o):
        _, dev = peer(o)
        pl.semaphore_signal(barrier, inc=1, device_id=dev, device_id_type=MESH)

    lane = iota((1, 128), 1)
    low = lane < 64
    low32 = jnp.broadcast_to(low, (32, 128))
    low64 = jnp.broadcast_to(low, (64, 128))

    def swap(a):
        return pltpu.roll(a, 64, 1)

    @pl.loop(0, 8)
    def _(c):
        r = iota((128, 512), 0)
        col = iota((128, 512), 1) + c * 512
        hit = ((col >> 6) == (r & 63)) & ((col & 63) == 63 * (r >> 6))
        sel_ref[:, pl.ds(pl.multiple_of(c * 512, 512), 512)] = jnp.where(hit, 1.0, 0.0).astype(bf16)

    fcopy.wait()
    mcopy.wait()
    fm0t = face_ref[0]
    fm1t = face_ref[1]
    r64 = iota((64, 64), 0)
    c64 = iota((64, 64), 1)
    eye64 = jnp.where(r64 == c64, 1.0, 0.0)
    qm = jnp.where(c64 == 2 * (r64 & 31) + (r64 >> 5), 1.0, 0.0)
    dup = jnp.where((iota((64, 128), 1) & 63) == iota((64, 128), 0), 1.0, 0.0)
    dupt = jnp.where((iota((128, 64), 0) & 63) == iota((128, 64), 1), 1.0, 0.0)
    eye128 = jnp.where(iota((128, 128), 0) == iota((128, 128), 1), 1.0, 0.0)
    fm0pt = nn(qm, fm0t)
    fm0 = nt(eye128, fm0t)
    fm0p = nt(eye128, fm0pt)
    fm11 = nt(eye128, jnp.concatenate([fm1t, fm1t], axis=0))

    mapf = [(map_ref[f] & 127).astype(f32) for f in range(6)]
    mapf = jnp.concatenate(mapf + [jnp.zeros((2, 128), f32)], axis=0)
    mapt = nt(eye128, mapf)
    lanef = iota((128, 128), 1).astype(f32)

    xcopy.wait()
    for q in range(T):
        s_ref[q * 8 : q * 8 + 8, :] = x_ref[0:8, q * 128 : q * 128 + 128]
        s_ref[256 + q * 8 : 256 + q * 8 + 8, :] = x_ref[56:64, q * 128 : q * 128 + 128]
    y0 = s_ref[pl.ds(0, 32, stride=8), :]
    y1 = s_ref[pl.ds(263, 32, stride=8), :]
    f01 = jnp.concatenate([jnp.where(low32, y0, swap(y1)), jnp.where(low32, swap(y0), y1)], axis=0)
    f23 = jnp.where(low64, x_ref[:, :128], x_ref[:, 31 * 128 :])
    xh, xl = split(x_ref[...])
    f45 = mmt(jnp.concatenate([xh, xl], axis=0), sel_ref[...])
    f45 = f45[:64] + f45[64:]

    rows = []
    for pair, (left, plane) in enumerate(((fm0p, f01), (fm0, f23), (fm0, f45))):
        u = mm(left3(left), rows3(plane)) * fm11
        for half in range(2):
            keep = low if half == 0 else jnp.logical_not(low)
            val = jnp.sum(jnp.where(keep, u, 0.0), axis=1, keepdims=True)
            f = 2 * pair + half
            place = mapt[:, f : f + 1] == lanef
            rows.append(jnp.sum(jnp.where(place, val, 0.0), axis=0, keepdims=True))
    mine = jnp.concatenate(rows + [jnp.zeros((2, 128), f32)], axis=0)
    send1_ref[...] = mine
    ag_ref[me] = mine

    pl.semaphore_wait(barrier, n - 1)

    @pl.loop(1, n)
    def _(o):
        _, dev = peer(o)
        pltpu.make_async_remote_copy(src_ref=send1_ref, dst_ref=ag_ref.at[me], send_sem=ag_s, recv_sem=ag_r,
                                     device_id=dev, device_id_type=MESH).start()

    ocopy.wait()
    m0, m1, m2 = modes_ref[0], modes_ref[1], modes_ref[2]
    am_ref[0] = left3(m0)
    am_ref[1] = left3(nt(eye64, m0))
    am_ref[2] = left3(nt(nn(qm, m1), qm))
    am_ref[3] = left3(nt(nt(qm, m1), qm))
    block = (iota((128, 128), 0) >> 6) == (iota((128, 128), 1) >> 6)
    kw_ref[0] = lanes_weights(jnp.where(block, nn(nt(dupt, m2), dup), 0.0))
    kw_ref[1] = lanes_weights(jnp.where(block, nn(dupt, nn(m2, dup)), 0.0))

    @pl.loop(0, T // CH)
    def _(c):
        base = pl.multiple_of(c * (CH * 128), CH * 128)
        y = mm(am_ref[0], rows3(x_ref[:, pl.ds(base, CH * 128)]))
        stacked = jnp.concatenate([y[:, g * 128 : g * 128 + 128] for g in range(CH)], axis=0)
        s_ref[pl.ds(pl.multiple_of(c * (CH * 64), CH * 64), CH * 64), :] = lane_transform(stacked, kw_ref[0])

    wcopy.wait()
    for q in range(T):
        z_ref[q * 64 : q * 64 + 64, :] = w_ref[:, q * 128 : q * 128 + 128]

    def turned(ref, u):
        a = ref[pl.ds(u, 32, stride=64), :]
        b = ref[pl.ds(u + 32, 32, stride=64), :]
        return jnp.concatenate([jnp.where(low32, a, swap(b)), jnp.where(low32, swap(a), b)], axis=0)

    def middle(c, acc):
        fwd = jnp.concatenate([turned(s_ref, c * CH + g) for g in range(CH)], axis=1)
        wts = jnp.concatenate([turned(z_ref, c * CH + g) for g in range(CH)], axis=1)
        v = mm(am_ref[2], rows3(fwd))
        wv = wts * v
        prod = wv * v
        for g in range(CH):
            acc = acc + prod[:, g * 128 : g * 128 + 128]
        y = mm(am_ref[3], rows3(wv))
        for g in range(CH):
            p_ref[pl.ds(pl.multiple_of(64 + (c * CH + g) * 64, 64), 64), :] = y[:, g * 128 : g * 128 + 128]
        return acc

    gacc = lax.fori_loop(0, T // CH, middle, jnp.zeros((64, 128), f32))

    lcopy.wait()
    cols = cols_ref[...]
    nrow = cols.shape[0]
    nz = cols.shape[1]
    wide_cols = jnp.concatenate([jnp.broadcast_to(cols[i : i + 1, :], (nz, nz)) for i in range(nrow)], axis=0)
    kk = nrow * nz
    pick_diag = iota((kk, nz), 1) == (iota((kk, nz), 0) & (nz - 1))
    colv = jnp.sum(jnp.where(pick_diag, wide_cols.astype(f32), 0.0), axis=1, keepdims=True)
    r = iota((1, n * 8), 1)
    d = r >> 3
    f = r & 7
    own = nrow * d + f
    own = jnp.where((f == 0) & (d >= ncg), nrow * (d - ncg) + 1, own)
    own = jnp.where((f == 2) & (lax.rem(d, ncg) > 0), nrow * (d - 1) + 3, own)
    own = jnp.where(f >= 6, -1, own).astype(f32)
    g1 = jnp.where(colv == own, 1.0, 0.0)
    g1 = jnp.concatenate([g1, jnp.zeros((128 - kk, n * 8), f32)], axis=0)

    pltpu.make_async_copy(ag_ref.at[pl.ds(0, n - 1)], ag_ref.at[pl.ds(0, n - 1)], ag_r).wait()
    picked = nn(g1, ag_ref[...].reshape(n * 8, 128))
    pick_ref[...] = picked[:kk].reshape(nrow, nz, 128)
    bcopy.wait()
    spread_ref[...] = jnp.zeros_like(spread_ref)

    def coarse_row(i, acc):
        pk = pick_ref[i]
        tot = blk_ref[i, 0] * pk[0:1]
        for k in range(1, nz):
            tot = tot + blk_ref[i, k] * pk[k : k + 1]
        img = jnp.sum(tot, axis=1, keepdims=True)
        out = [jnp.sum(blk_ref[i, k] * img, axis=0, keepdims=True) for k in range(nz)]
        spread_ref[i] = jnp.concatenate(out, axis=0)
        return acc + img * img

    iacc = lax.fori_loop(0, nrow, coarse_row, jnp.zeros((128, 1), f32))
    gpart = jnp.sum(iacc, keepdims=True) + jnp.sum(gacc, keepdims=True)
    back = nn(g1.T, spread_ref[...].reshape(128, 128))
    back = jnp.where((iota((n * 8, 128), 0) & 7) == 6, gpart, back)
    a2s_ref[...] = back.reshape(n, 8, 128)
    a2r_ref[me] = a2s_ref[me]

    @pl.loop(1, n)
    def _(o):
        dd, dev = peer(o)
        pltpu.make_async_remote_copy(src_ref=a2s_ref.at[dd], dst_ref=a2r_ref.at[me], send_sem=a2_s, recv_sem=a2_r,
                                     device_id=dev, device_id_type=MESH).start()

    @pl.loop(0, T // CH)
    def _(c):
        tiles = []
        for g in range(CH):
            a = p_ref[pl.ds(64 + c * CH + g, 32, stride=64), :]
            b = p_ref[pl.ds(96 + c * CH + g, 32, stride=64), :]
            tiles.append(jnp.where(low32, a, swap(b)))
            tiles.append(jnp.where(low32, swap(a), b))
        k = lane_transform(jnp.concatenate(tiles, axis=0), kw_ref[1])
        y = jnp.concatenate([k[g * 64 : g * 64 + 64] for g in range(CH)], axis=1)
        y = mm(am_ref[1], rows3(y))
        for g in range(CH):
            s_ref[pl.ds(pl.multiple_of((c * CH + g) * 64, 64), 64), :] = y[:, g * 128 : g * 128 + 128]

    pltpu.make_async_copy(a2r_ref.at[pl.ds(0, n - 1)], a2r_ref.at[pl.ds(0, n - 1)], a2_r).wait()
    backs = jnp.sum(a2r_ref[...], axis=0)
    gamma = backs[6:7, :]
    corr = []
    for f in range(6):
        place = mapt[:, f : f + 1] == lanef
        corr.append(jnp.sum(jnp.where(place, backs[f : f + 1], 0.0), axis=1, keepdims=True))
    e01 = mm(left3(fm0pt), rows3(jnp.where(low, corr[0], corr[1]) * fm11))
    e23 = mm(left3(fm0t), rows3(jnp.where(low, corr[2], corr[3]) * fm11))
    e45 = mm(left3(fm0t), rows3(jnp.where(low, corr[4], corr[5]) * fm11))
    eh, el = split(e45)
    eh = jnp.concatenate([eh, el], axis=0)

    @pl.loop(0, T // CH)
    def _(c):
        base = pl.multiple_of(c * (CH * 128), CH * 128)
        add = mm(eh, sel_ref[:, pl.ds(base, CH * 128)])
        for g in range(CH):
            at = pl.multiple_of((c * CH + g) * 64, 64)
            tile = add[:64, g * 128 : g * 128 + 128] + add[64:, g * 128 : g * 128 + 128]
            p_ref[pl.ds(at + 64, 64), :] = s_ref[pl.ds(at, 64), :] + tile

    p_ref[64:128, :] += jnp.where(low64, e23, 0.0)
    p_ref[T * 64 : T * 64 + 64, :] += jnp.where(low64, 0.0, e23)
    top, bottom = e01[:32], e01[32:]
    edge0 = p_ref[pl.ds(64, 32, stride=64), :] + jnp.where(low32, top, swap(bottom))
    edge1 = p_ref[pl.ds(64 + 63, 32, stride=64), :] + jnp.where(low32, swap(top), bottom)
    p_ref[pl.ds(64, 32, stride=64), :] = edge0
    p_ref[pl.ds(64 + 63, 32, stride=64), :] = edge1

    his_ref[0] = edge0
    his_ref[1] = edge1
    hjs_ref[0] = p_ref[64:128, :]
    hjs_ref[1] = p_ref[T * 64 : T * 64 + 64, :]

    sends = (
        (s > 0, s < nsub - 1, (s - 1, t), his_ref, hi_ref, 0, 1, 0),
        (s < nsub - 1, s > 0, (s + 1, t), his_ref, hi_ref, 1, 0, 1),
        (t > 0, t < ncg - 1, (s, t - 1), hjs_ref, hj_ref, 0, 1, 2),
        (t < ncg - 1, t > 0, (s, t + 1), hjs_ref, hj_ref, 1, 0, 3),
    )

    def halo(dev, src, dst, a, b, k):
        return pltpu.make_async_remote_copy(src_ref=src.at[a], dst_ref=dst.at[b], send_sem=h_s.at[k],
                                            recv_sem=h_r.at[k], device_id=dev, device_id_type=MESH)

    for does, gets, dev, src, dst, a, b, k in sends:
        @pl.when(does)
        def _():
            halo(dev, src, dst, a, b, k).start()

        @pl.when(jnp.logical_not(gets))
        def _():
            dst[b] = jnp.zeros(dst.shape[1:], f32)

    ccopy.wait()
    p_ref[0:64, :] = jnp.zeros((64, 128), f32)
    p_ref[(T + 1) * 64 : (T + 2) * 64, :] = jnp.zeros((64, 128), f32)

    row = iota((64, 128), 0)
    kpos = iota((64, 128), 1) & 63

    def stencil(q, acc):
        at = pl.multiple_of(q * 64, 64)
        x = p_ref[pl.ds(at + 64, 64), :]
        here = swap(x)
        before = swap(p_ref[pl.ds(at, 64), :])
        after = swap(p_ref[pl.ds(at + 128, 64), :])
        second = here + jnp.where(low64, before, after)
        up = jnp.where(row == 0, 0.0, pltpu.roll(x, 1, 0))
        down = jnp.where(row == 63, 0.0, pltpu.roll(x, 63, 0))
        third = jnp.where(kpos == 0, 0.0, pltpu.roll(x, 1, 1)) + jnp.where(kpos == 63, 0.0, pltpu.roll(x, 127, 1))
        cols_at = pl.ds(pl.multiple_of(q * 128, 128), 128)
        img = (cap_ref[:, cols_at] + 8.2) * x - (up + down) - 0.6 * second - 2.5 * third
        img_out[:, cols_at] = img
        p_out[:, cols_at] = x
        return acc + x * img

    cacc = lax.fori_loop(0, T, stencil, jnp.zeros((64, 128), f32), unroll=2)
    for does, gets, dev, src, dst, a, b, k in sends:
        @pl.when(gets)
        def _():
            halo(dev, src, dst, a, b, k).wait_recv()

    fix0 = 0.6 * jnp.where(low64, swap(hj_ref[0]), 0.0)
    fix1 = 0.6 * jnp.where(low64, 0.0, swap(hj_ref[1]))
    cacc = cacc - hjs_ref[0] * fix0 - hjs_ref[1] * fix1
    csum = his_ref[0] * hi_ref[0] + his_ref[1] * hi_ref[1]
    cpart = jnp.sum(cacc, axis=0, keepdims=True) - jnp.sum(csum, axis=0, keepdims=True)
    cs_ref[...] = cpart
    cr_ref[me] = cpart

    @pl.loop(1, n)
    def _(o):
        _, dev = peer(o)
        pltpu.make_async_remote_copy(src_ref=cs_ref, dst_ref=cr_ref.at[me], send_sem=c_s, recv_sem=c_r,
                                     device_id=dev, device_id_type=MESH).start()

    img_out[:, :128] = img_out[:, :128] - fix0
    img_out[:, (T - 1) * 128 :] = img_out[:, (T - 1) * 128 :] - fix1
    for q in range(T):
        at = slice(q * 128, q * 128 + 128)
        img_out[0:1, at] = img_out[0:1, at] - hi_ref[0, q : q + 1, :]
        img_out[63:64, at] = img_out[63:64, at] - hi_ref[1, q : q + 1, :]

    pltpu.make_async_copy(cr_ref.at[pl.ds(0, n - 1)], cr_ref.at[pl.ds(0, n - 1)], c_r).wait()
    curv = jnp.sum(jnp.sum(cr_ref[...], axis=0), axis=1, keepdims=True)
    alpha_out[...] = gamma[:, 0:1] / curv

    pltpu.make_async_copy(ag_ref.at[pl.ds(0, n - 1)], ag_ref.at[pl.ds(0, n - 1)], ag_s).wait()
    pltpu.make_async_copy(a2r_ref.at[pl.ds(0, n - 1)], a2r_ref.at[pl.ds(0, n - 1)], a2_s).wait()
    pltpu.make_async_copy(cr_ref.at[pl.ds(0, n - 1)], cr_ref.at[pl.ds(0, n - 1)], c_s).wait()
    for does, gets, dev, src, dst, a, b, k in sends:
        @pl.when(does)
        def _():
            halo(dev, src, dst, a, b, k).wait_send()


def body(nsub, ncg, source, capacity, fd_weights, fd_modes, face_modes, coarse_map, fsai_cols, fsai_blocks):
    n = nsub * ncg
    nrow, nz = fsai_cols.shape
    vm = pl.BlockSpec(memory_space=pltpu.VMEM)
    hbm = pl.BlockSpec(memory_space=pltpu.HBM)
    field = jax.ShapeDtypeStruct(source.shape, f32)
    V = pltpu.VMEM
    dma = pltpu.SemaphoreType.DMA
    p, img, alpha = pl.pallas_call(
        functools.partial(kernel, nsub, ncg),
        out_shape=(field, field, jax.ShapeDtypeStruct((1, 1), f32)),
        in_specs=[hbm] * 8,
        out_specs=(vm, vm, vm),
        scratch_shapes=[
            V(source.shape, f32),
            V(fd_modes.shape, f32),
            V((2, 64, 128), f32),
            V((6, 1, 128), jnp.int32),
            V(fsai_cols.shape, jnp.int32),
            V((T * 64, 128), f32),
            V((T * 64, 128), f32),
            V((64, T * 128), f32),
            V(((T + 2) * 64, 128), f32),
            V((64, T * 128), f32),
            V(fsai_blocks.shape, f32),
            V((128, T * 128), bf16),
            V((4, 64, 192), bf16),
            V((2, 256, 256), bf16),
            V((n, 8, 128), f32),
            V((8, 128), f32),
            V((n, 8, 128), f32),
            V((n, 8, 128), f32),
            V((nrow, nz, 128), f32),
            V((128 // nz, nz, 128), f32),
            V((2, 32, 128), f32),
            V((2, 32, 128), f32),
            V((2, 64, 128), f32),
            V((2, 64, 128), f32),
            V((1, 128), f32),
            V((n, 1, 128), f32),
            dma((8,)),
            dma, dma, dma, dma,
            dma((4,)), dma((4,)),
            dma, dma,
        ],
        compiler_params=pltpu.CompilerParams(collective_id=0, has_side_effects=True,
                                             vmem_limit_bytes=48 * 1024 * 1024),
        cost_estimate=pl.CostEstimate(flops=10**9, bytes_accessed=8 * 2**20, transcendentals=0),
        name="step",
    )(*(pltpu.with_memory_space_constraint(v, pltpu.HBM) for v in (
        source, fd_modes, jnp.swapaxes(face_modes, 1, 2), coarse_map.reshape(-1, 1, coarse_map.shape[-1]),
        fsai_cols, capacity, fd_weights, fsai_blocks)))
    a = alpha[0, 0]
    return a * p, source - a * img


def solution(mesh):
    in_specs = (
        P("sub", "cgrp"),
        P("sub", "cgrp"),
        P("sub", "cgrp"),
        P(),
        P(),
        P("sub", "cgrp", None, None),
        P(("sub", "cgrp"), None),
        P(("sub", "cgrp"), None, None, None),
    )
    out_specs = (P("sub", "cgrp"), P("sub", "cgrp"))
    step = functools.partial(body, mesh.shape["sub"], mesh.shape["cgrp"])
    return jax.shard_map(step, mesh=mesh, in_specs=in_specs, out_specs=out_specs, check_vma=False)
```

```python
import functools
import jax
import jax.numpy as jnp
from jax import lax
from jax.experimental import pallas as pl
from jax.experimental.pallas import tpu as pltpu
from jax.sharding import PartitionSpec as P

C = 64
T = 32
CH = 8
f32 = jnp.float32
bf16 = jnp.bfloat16
HI = lax.Precision.HIGHEST
MESH = pl.DeviceIdType.MESH


def nn(a, b):
    return lax.dot_general(a, b, (((1,), (0,)), ((), ())), precision=HI, preferred_element_type=f32)


def nt(a, b):
    return lax.dot_general(a, b, (((1,), (1,)), ((), ())), precision=HI, preferred_element_type=f32)


def mm(a, b):
    return lax.dot_general(a, b, (((1,), (0,)), ((), ())), preferred_element_type=f32)


def mmt(a, b):
    return lax.dot_general(a, b, (((1,), (1,)), ((), ())), preferred_element_type=f32)


def split(x):
    hi = x.astype(bf16)
    return hi, (x - hi.astype(f32)).astype(bf16)


def iota(shape, dim):
    return lax.broadcasted_iota(jnp.int32, shape, dim)


def left3(m):
    hi, lo = split(m)
    return jnp.concatenate([hi, lo, hi], axis=1)


def rows3(x):
    hi, lo = split(x)
    return jnp.concatenate([hi, hi, lo], axis=0)


def lanes_weights(k):
    hi, lo = split(k)
    top = jnp.concatenate([hi, lo], axis=1)
    bottom = jnp.concatenate([hi, jnp.zeros_like(lo)], axis=1)
    return jnp.concatenate([top, bottom], axis=0)


def lane_transform(x, w):
    hi, lo = split(x)
    r = mm(jnp.concatenate([hi, lo], axis=1), w)
    return r[:, :128] + r[:, 128:]


def kernel(nsub, ncg, x_any, modes_any, face_any, map_any, cols_any, cap_any, wt_any, blk_any,
           p_out, img_out, alpha_out,
           x_ref, modes_ref, face_ref, map_ref, cols_ref,
           s_ref, z_ref, w_ref, p_ref, cap_ref, blk_ref, sel_ref, am_ref, kw_ref,
           ag_ref, send1_ref, a2s_ref, a2r_ref, pick_ref, spread_ref,
           hi_ref, his_ref, hj_ref, hjs_ref, cs_ref, cr_ref,
           dsem, ag_s, ag_r, a2_s, a2_r, h_s, h_r, c_s, c_r):
    n = nsub * ncg
    s = lax.axis_index("sub")
    t = lax.axis_index("cgrp")
    me = s * ncg + t

    def peer(o):
        d = lax.rem(me + o, n)
        return d, (lax.div(d, ncg), lax.rem(d, ncg))

    early = []
    for k, (src, dst) in enumerate(((face_any, face_ref), (map_any, map_ref), (x_any, x_ref),
                                    (modes_any, modes_ref), (cols_any, cols_ref),
                                    (wt_any, w_ref), (blk_any, blk_ref), (cap_any, cap_ref))):
        early.append(pltpu.make_async_copy(src, dst, dsem.at[k]))
        early[-1].start()
    fcopy, mcopy, xcopy, ocopy, lcopy, wcopy, bcopy, ccopy = early

    def peers(step):
        if n > 32:
            pl.loop(1, n)(step)
        else:
            for o in range(1, n):
                step(o)

    barrier = pltpu.get_barrier_semaphore()

    @pl.loop(1, n)
    def _(o):
        _, dev = peer(o)
        pl.semaphore_signal(barrier, inc=1, device_id=dev, device_id_type=MESH)

    lane = iota((1, 128), 1)
    low = lane < 64
    low32 = jnp.broadcast_to(low, (32, 128))
    low64 = jnp.broadcast_to(low, (64, 128))

    def swap(a):
        return pltpu.roll(a, 64, 1)

    @pl.loop(0, 8)
    def _(c):
        r = iota((128, 512), 0)
        col = iota((128, 512), 1) + c * 512
        hit = ((col >> 6) == (r & 63)) & ((col & 63) == 63 * (r >> 6))
        sel_ref[:, pl.ds(pl.multiple_of(c * 512, 512), 512)] = jnp.where(hit, 1.0, 0.0).astype(bf16)

    fcopy.wait()
    mcopy.wait()
    fm0t = face_ref[0]
    fm1t = face_ref[1]
    r64 = iota((64, 64), 0)
    c64 = iota((64, 64), 1)
    eye64 = jnp.where(r64 == c64, 1.0, 0.0)
    qm = jnp.where(c64 == 2 * (r64 & 31) + (r64 >> 5), 1.0, 0.0)
    dup = jnp.where((iota((64, 128), 1) & 63) == iota((64, 128), 0), 1.0, 0.0)
    dupt = jnp.where((iota((128, 64), 0) & 63) == iota((128, 64), 1), 1.0, 0.0)
    eye128 = jnp.where(iota((128, 128), 0) == iota((128, 128), 1), 1.0, 0.0)
    fm0pt = nn(qm, fm0t)
    fm0 = fm0t.T
    fm0p = fm0pt.T
    fm11 = jnp.concatenate([fm1t, fm1t], axis=0).T

    mapf = [(map_ref[f] & 127).astype(f32) for f in range(6)]
    mapf = jnp.concatenate(mapf + [jnp.zeros((2, 128), f32)], axis=0)
    mapt = mmt(eye128.astype(bf16), mapf.astype(bf16))
    lanef = iota((128, 128), 1).astype(f32)

    xcopy.wait()
    for q in range(T):
        s_ref[q * 8 : q * 8 + 8, :] = x_ref[0:8, q * 128 : q * 128 + 128]
        s_ref[256 + q * 8 : 256 + q * 8 + 8, :] = x_ref[56:64, q * 128 : q * 128 + 128]
    y0 = s_ref[pl.ds(0, 32, stride=8), :]
    y1 = s_ref[pl.ds(263, 32, stride=8), :]
    f01 = jnp.concatenate([jnp.where(low32, y0, swap(y1)), jnp.where(low32, swap(y0), y1)], axis=0)
    f23 = jnp.where(low64, x_ref[:, :128], x_ref[:, 31 * 128 :])
    xh, xl = split(x_ref[...])
    f45 = mmt(jnp.concatenate([xh, xl], axis=0), sel_ref[...])
    f45 = f45[:64] + f45[64:]

    rows = []
    for pair, (left, plane) in enumerate(((fm0p, f01), (fm0, f23), (fm0, f45))):
        u = mm(left3(left), rows3(plane)) * fm11
        for half in range(2):
            keep = low if half == 0 else jnp.logical_not(low)
            val = jnp.sum(jnp.where(keep, u, 0.0), axis=1, keepdims=True)
            f = 2 * pair + half
            place = mapt[:, f : f + 1] == lanef
            rows.append(jnp.sum(jnp.where(place, val, 0.0), axis=0, keepdims=True))
    mine = jnp.concatenate(rows + [jnp.zeros((2, 128), f32)], axis=0)
    send1_ref[...] = mine
    ag_ref[me] = mine

    pl.semaphore_wait(barrier, n - 1)

    @peers
    def _(o):
        _, dev = peer(o)
        pltpu.make_async_remote_copy(src_ref=send1_ref, dst_ref=ag_ref.at[me], send_sem=ag_s, recv_sem=ag_r,
                                     device_id=dev, device_id_type=MESH).start()

    ocopy.wait()
    m0, m1, m2 = modes_ref[0], modes_ref[1], modes_ref[2]
    am_ref[0] = left3(m0)
    am_ref[1] = left3(nt(eye64, m0))
    am_ref[2] = left3(nt(nn(qm, m1), qm))
    am_ref[3] = left3(nt(nt(qm, m1), qm))
    block = (iota((128, 128), 0) >> 6) == (iota((128, 128), 1) >> 6)
    kw_ref[0] = lanes_weights(jnp.where(block, nn(nt(dupt, m2), dup), 0.0))
    kw_ref[1] = lanes_weights(jnp.where(block, nn(dupt, nn(m2, dup)), 0.0))

    @pl.loop(0, T // CH)
    def _(c):
        base = pl.multiple_of(c * (CH * 128), CH * 128)
        y = mm(am_ref[0], rows3(x_ref[:, pl.ds(base, CH * 128)]))
        stacked = jnp.concatenate([y[:, g * 128 : g * 128 + 128] for g in range(CH)], axis=0)
        s_ref[pl.ds(pl.multiple_of(c * (CH * 64), CH * 64), CH * 64), :] = lane_transform(stacked, kw_ref[0])

    wcopy.wait()
    for q in range(T):
        z_ref[q * 64 : q * 64 + 64, :] = w_ref[:, q * 128 : q * 128 + 128]

    def turned(ref, u):
        a = ref[pl.ds(u, 32, stride=64), :]
        b = ref[pl.ds(u + 32, 32, stride=64), :]
        return jnp.concatenate([jnp.where(low32, a, swap(b)), jnp.where(low32, swap(a), b)], axis=0)

    def middle(c, acc):
        fwd = jnp.concatenate([turned(s_ref, c * CH + g) for g in range(CH)], axis=1)
        wts = jnp.concatenate([turned(z_ref, c * CH + g) for g in range(CH)], axis=1)
        v = mm(am_ref[2], rows3(fwd))
        wv = wts * v
        prod = wv * v
        for g in range(CH):
            acc = acc + prod[:, g * 128 : g * 128 + 128]
        y = mm(am_ref[3], rows3(wv))
        for g in range(CH):
            p_ref[pl.ds(pl.multiple_of(64 + (c * CH + g) * 64, 64), 64), :] = y[:, g * 128 : g * 128 + 128]
        return acc

    gacc = lax.fori_loop(0, T // CH, middle, jnp.zeros((64, 128), f32))

    lcopy.wait()
    cols = cols_ref[...]
    nrow = cols.shape[0]
    nz = cols.shape[1]
    wide_cols = jnp.concatenate([jnp.broadcast_to(cols[i : i + 1, :], (nz, nz)) for i in range(nrow)], axis=0)
    kk = nrow * nz
    pick_diag = iota((kk, nz), 1) == (iota((kk, nz), 0) & (nz - 1))
    colv = jnp.sum(jnp.where(pick_diag, wide_cols.astype(f32), 0.0), axis=1, keepdims=True)
    r = iota((1, n * 8), 1)
    d = r >> 3
    f = r & 7
    own = nrow * d + f
    own = jnp.where((f == 0) & (d >= ncg), nrow * (d - ncg) + 1, own)
    own = jnp.where((f == 2) & (lax.rem(d, ncg) > 0), nrow * (d - 1) + 3, own)
    own = jnp.where(f >= 6, -1, own).astype(f32)
    g1 = jnp.where(colv == own, 1.0, 0.0)
    g1 = jnp.concatenate([g1, jnp.zeros((128 - kk, n * 8), f32)], axis=0)

    g2 = g1.T.astype(bf16)
    g2 = jnp.concatenate([g2, g2], axis=1)
    g1 = g1.astype(bf16)

    pltpu.make_async_copy(ag_ref.at[pl.ds(0, n - 1)], ag_ref.at[pl.ds(0, n - 1)], ag_r).wait()
    th, tl = split(ag_ref[...].reshape(n * 8, 128))
    picked = mm(g1, th) + mm(g1, tl)
    pick_ref[...] = picked[:kk].reshape(nrow, nz, 128)
    bcopy.wait()
    spread_ref[...] = jnp.zeros_like(spread_ref)

    def coarse_row(i, acc):
        pk = pick_ref[i]
        tot = blk_ref[i, 0] * pk[0:1]
        for k in range(1, nz):
            tot = tot + blk_ref[i, k] * pk[k : k + 1]
        img = jnp.sum(tot, axis=1, keepdims=True)
        out = [jnp.sum(blk_ref[i, k] * img, axis=0, keepdims=True) for k in range(nz)]
        spread_ref[i] = jnp.concatenate(out, axis=0)
        return acc + img * img

    iacc = lax.fori_loop(0, nrow, coarse_row, jnp.zeros((128, 1), f32))
    gpart = jnp.sum(iacc, keepdims=True) + jnp.sum(gacc, keepdims=True)
    back = mm(g2, jnp.concatenate(split(spread_ref[...].reshape(128, 128)), axis=0))
    back = jnp.where((iota((n * 8, 128), 0) & 7) == 6, gpart, back)
    a2s_ref[...] = back.reshape(n, 8, 128)
    a2r_ref[me] = a2s_ref[me]

    @peers
    def _(o):
        dd, dev = peer(o)
        pltpu.make_async_remote_copy(src_ref=a2s_ref.at[dd], dst_ref=a2r_ref.at[me], send_sem=a2_s, recv_sem=a2_r,
                                     device_id=dev, device_id_type=MESH).start()

    @pl.loop(0, T // CH)
    def _(c):
        tiles = []
        for g in range(CH):
            a = p_ref[pl.ds(64 + c * CH + g, 32, stride=64), :]
            b = p_ref[pl.ds(96 + c * CH + g, 32, stride=64), :]
            tiles.append(jnp.where(low32, a, swap(b)))
            tiles.append(jnp.where(low32, swap(a), b))
        k = lane_transform(jnp.concatenate(tiles, axis=0), kw_ref[1])
        y = jnp.concatenate([k[g * 64 : g * 64 + 64] for g in range(CH)], axis=1)
        y = mm(am_ref[1], rows3(y))
        for g in range(CH):
            s_ref[pl.ds(pl.multiple_of((c * CH + g) * 64, 64), 64), :] = y[:, g * 128 : g * 128 + 128]

    pltpu.make_async_copy(a2r_ref.at[pl.ds(0, n - 1)], a2r_ref.at[pl.ds(0, n - 1)], a2_r).wait()
    backs = jnp.sum(a2r_ref[...], axis=0)
    gamma = backs[6:7, :]
    corr = []
    for f in range(6):
        place = mapt[:, f : f + 1] == lanef
        corr.append(jnp.sum(jnp.where(place, backs[f : f + 1], 0.0), axis=1, keepdims=True))
    e01 = mm(left3(fm0pt), rows3(jnp.where(low, corr[0], corr[1]) * fm11))
    e23 = mm(left3(fm0t), rows3(jnp.where(low, corr[2], corr[3]) * fm11))
    e45 = mm(left3(fm0t), rows3(jnp.where(low, corr[4], corr[5]) * fm11))
    eh, el = split(e45)
    eh = jnp.concatenate([eh, el], axis=0)

    @pl.loop(0, T // CH)
    def _(c):
        base = pl.multiple_of(c * (CH * 128), CH * 128)
        add = mm(eh, sel_ref[:, pl.ds(base, CH * 128)])
        for g in range(CH):
            at = pl.multiple_of((c * CH + g) * 64, 64)
            tile = add[:64, g * 128 : g * 128 + 128] + add[64:, g * 128 : g * 128 + 128]
            p_ref[pl.ds(at + 64, 64), :] = s_ref[pl.ds(at, 64), :] + tile

    p_ref[64:128, :] += jnp.where(low64, e23, 0.0)
    p_ref[T * 64 : T * 64 + 64, :] += jnp.where(low64, 0.0, e23)
    top, bottom = e01[:32], e01[32:]
    edge0 = p_ref[pl.ds(64, 32, stride=64), :] + jnp.where(low32, top, swap(bottom))
    edge1 = p_ref[pl.ds(64 + 63, 32, stride=64), :] + jnp.where(low32, swap(top), bottom)
    p_ref[pl.ds(64, 32, stride=64), :] = edge0
    p_ref[pl.ds(64 + 63, 32, stride=64), :] = edge1

    his_ref[0] = edge0
    his_ref[1] = edge1
    hjs_ref[0] = p_ref[64:128, :]
    hjs_ref[1] = p_ref[T * 64 : T * 64 + 64, :]

    sends = (
        (s > 0, s < nsub - 1, (s - 1, t), his_ref, hi_ref, 0, 1, 0),
        (s < nsub - 1, s > 0, (s + 1, t), his_ref, hi_ref, 1, 0, 1),
        (t > 0, t < ncg - 1, (s, t - 1), hjs_ref, hj_ref, 0, 1, 2),
        (t < ncg - 1, t > 0, (s, t + 1), hjs_ref, hj_ref, 1, 0, 3),
    )

    def halo(dev, src, dst, a, b, k):
        return pltpu.make_async_remote_copy(src_ref=src.at[a], dst_ref=dst.at[b], send_sem=h_s.at[k],
                                            recv_sem=h_r.at[k], device_id=dev, device_id_type=MESH)

    for does, gets, dev, src, dst, a, b, k in sends:
        @pl.when(does)
        def _():
            halo(dev, src, dst, a, b, k).start()

        @pl.when(jnp.logical_not(gets))
        def _():
            dst[b] = jnp.zeros(dst.shape[1:], f32)

    ccopy.wait()
    p_ref[0:64, :] = jnp.zeros((64, 128), f32)
    p_ref[(T + 1) * 64 : (T + 2) * 64, :] = jnp.zeros((64, 128), f32)

    row = iota((64, 128), 0)
    kpos = iota((64, 128), 1) & 63

    def stencil(q, acc):
        at = pl.multiple_of(q * 64, 64)
        x = p_ref[pl.ds(at + 64, 64), :]
        here = swap(x)
        before = swap(p_ref[pl.ds(at, 64), :])
        after = swap(p_ref[pl.ds(at + 128, 64), :])
        second = here + jnp.where(low64, before, after)
        up = jnp.where(row == 0, 0.0, pltpu.roll(x, 1, 0))
        down = jnp.where(row == 63, 0.0, pltpu.roll(x, 63, 0))
        third = jnp.where(kpos == 0, 0.0, pltpu.roll(x, 1, 1)) + jnp.where(kpos == 63, 0.0, pltpu.roll(x, 127, 1))
        cols_at = pl.ds(pl.multiple_of(q * 128, 128), 128)
        img = (cap_ref[:, cols_at] + 8.2) * x - (up + down) - 0.6 * second - 2.5 * third
        img_out[:, cols_at] = img
        p_out[:, cols_at] = x
        return acc + x * img

    cacc = lax.fori_loop(0, T, stencil, jnp.zeros((64, 128), f32), unroll=2)
    for does, gets, dev, src, dst, a, b, k in sends:
        @pl.when(gets)
        def _():
            halo(dev, src, dst, a, b, k).wait_recv()

    fix0 = 0.6 * jnp.where(low64, swap(hj_ref[0]), 0.0)
    fix1 = 0.6 * jnp.where(low64, 0.0, swap(hj_ref[1]))
    cacc = cacc - hjs_ref[0] * fix0 - hjs_ref[1] * fix1
    csum = his_ref[0] * hi_ref[0] + his_ref[1] * hi_ref[1]
    cpart = jnp.sum(cacc, axis=0, keepdims=True) - jnp.sum(csum, axis=0, keepdims=True)
    cs_ref[...] = cpart
    cr_ref[me] = cpart

    @peers
    def _(o):
        _, dev = peer(o)
        pltpu.make_async_remote_copy(src_ref=cs_ref, dst_ref=cr_ref.at[me], send_sem=c_s, recv_sem=c_r,
                                     device_id=dev, device_id_type=MESH).start()

    img_out[:, :128] = img_out[:, :128] - fix0
    img_out[:, (T - 1) * 128 :] = img_out[:, (T - 1) * 128 :] - fix1
    for q in range(T):
        at = slice(q * 128, q * 128 + 128)
        img_out[0:1, at] = img_out[0:1, at] - hi_ref[0, q : q + 1, :]
        img_out[63:64, at] = img_out[63:64, at] - hi_ref[1, q : q + 1, :]

    pltpu.make_async_copy(cr_ref.at[pl.ds(0, n - 1)], cr_ref.at[pl.ds(0, n - 1)], c_r).wait()
    curv = jnp.sum(jnp.sum(cr_ref[...], axis=0), axis=1, keepdims=True)
    alpha_out[...] = gamma[:, 0:1] / curv

    pltpu.make_async_copy(ag_ref.at[pl.ds(0, n - 1)], ag_ref.at[pl.ds(0, n - 1)], ag_s).wait()
    pltpu.make_async_copy(a2r_ref.at[pl.ds(0, n - 1)], a2r_ref.at[pl.ds(0, n - 1)], a2_s).wait()
    pltpu.make_async_copy(cr_ref.at[pl.ds(0, n - 1)], cr_ref.at[pl.ds(0, n - 1)], c_s).wait()
    for does, gets, dev, src, dst, a, b, k in sends:
        @pl.when(does)
        def _():
            halo(dev, src, dst, a, b, k).wait_send()


def body(nsub, ncg, source, capacity, fd_weights, fd_modes, face_modes, coarse_map, fsai_cols, fsai_blocks):
    n = nsub * ncg
    nrow, nz = fsai_cols.shape
    vm = pl.BlockSpec(memory_space=pltpu.VMEM)
    hbm = pl.BlockSpec(memory_space=pltpu.HBM)
    field = jax.ShapeDtypeStruct(source.shape, f32)
    V = pltpu.VMEM
    dma = pltpu.SemaphoreType.DMA
    p, img, alpha = pl.pallas_call(
        functools.partial(kernel, nsub, ncg),
        out_shape=(field, field, jax.ShapeDtypeStruct((1, 1), f32)),
        in_specs=[hbm] * 8,
        out_specs=(vm, vm, vm),
        scratch_shapes=[
            V(source.shape, f32),
            V(fd_modes.shape, f32),
            V((2, 64, 128), f32),
            V((6, 1, 128), jnp.int32),
            V(fsai_cols.shape, jnp.int32),
            V((T * 64, 128), f32),
            V((T * 64, 128), f32),
            V((64, T * 128), f32),
            V(((T + 2) * 64, 128), f32),
            V((64, T * 128), f32),
            V(fsai_blocks.shape, f32),
            V((128, T * 128), bf16),
            V((4, 64, 192), bf16),
            V((2, 256, 256), bf16),
            V((n, 8, 128), f32),
            V((8, 128), f32),
            V((n, 8, 128), f32),
            V((n, 8, 128), f32),
            V((nrow, nz, 128), f32),
            V((128 // nz, nz, 128), f32),
            V((2, 32, 128), f32),
            V((2, 32, 128), f32),
            V((2, 64, 128), f32),
            V((2, 64, 128), f32),
            V((1, 128), f32),
            V((n, 1, 128), f32),
            dma((8,)),
            dma, dma, dma, dma,
            dma((4,)), dma((4,)),
            dma, dma,
        ],
        compiler_params=pltpu.CompilerParams(collective_id=0, has_side_effects=True,
                                             vmem_limit_bytes=48 * 1024 * 1024),
        cost_estimate=pl.CostEstimate(flops=10**9, bytes_accessed=8 * 2**20, transcendentals=0),
        name="step",
    )(*(pltpu.with_memory_space_constraint(v, pltpu.HBM) for v in (
        source, fd_modes, jnp.swapaxes(face_modes, 1, 2), coarse_map.reshape(-1, 1, coarse_map.shape[-1]),
        fsai_cols, capacity, fd_weights, fsai_blocks)))
    a = alpha[0, 0]
    return a * p, source - a * img


def solution(mesh):
    in_specs = (
        P("sub", "cgrp"),
        P("sub", "cgrp"),
        P("sub", "cgrp"),
        P(),
        P(),
        P("sub", "cgrp", None, None),
        P(("sub", "cgrp"), None),
        P(("sub", "cgrp"), None, None, None),
    )
    out_specs = (P("sub", "cgrp"), P("sub", "cgrp"))
    step = functools.partial(body, mesh.shape["sub"], mesh.shape["cgrp"])
    return jax.shard_map(step, mesh=mesh, in_specs=in_specs, out_specs=out_specs, check_vma=False)
```

```python
import functools
import jax
import jax.numpy as jnp
from jax import lax
from jax.experimental import pallas as pl
from jax.experimental.pallas import tpu as pltpu
from jax.sharding import PartitionSpec as P

C = 64
T = 32
CH = 8
f32 = jnp.float32
bf16 = jnp.bfloat16
HI = lax.Precision.HIGHEST
MESH = pl.DeviceIdType.MESH


def nn(a, b):
    return lax.dot_general(a, b, (((1,), (0,)), ((), ())), precision=HI, preferred_element_type=f32)


def nt(a, b):
    return lax.dot_general(a, b, (((1,), (1,)), ((), ())), precision=HI, preferred_element_type=f32)


def mm(a, b):
    return lax.dot_general(a, b, (((1,), (0,)), ((), ())), preferred_element_type=f32)


def mmt(a, b):
    return lax.dot_general(a, b, (((1,), (1,)), ((), ())), preferred_element_type=f32)


def split(x):
    hi = x.astype(bf16)
    return hi, (x - hi.astype(f32)).astype(bf16)


def iota(shape, dim):
    return lax.broadcasted_iota(jnp.int32, shape, dim)


def left3(m):
    hi, lo = split(m)
    return jnp.concatenate([hi, lo, hi], axis=1)


def rows3(x):
    hi, lo = split(x)
    return jnp.concatenate([hi, hi, lo], axis=0)


def lanes_weights(k):
    hi, lo = split(k)
    top = jnp.concatenate([hi, lo], axis=1)
    bottom = jnp.concatenate([hi, jnp.zeros_like(lo)], axis=1)
    return jnp.concatenate([top, bottom], axis=0)


def lane_transform(x, w):
    hi, lo = split(x)
    r = mm(jnp.concatenate([hi, lo], axis=1), w)
    return r[:, :128] + r[:, 128:]


def kernel(nsub, ncg, x_any, modes_any, face_any, map_any, cols_any, cap_any, wt_any, blk_any,
           p_out, img_out, alpha_out,
           x_ref, modes_ref, face_ref, map_ref, cols_ref,
           s_ref, z_ref, w_ref, p_ref, cap_ref, blk_ref, sel_ref, am_ref, kw_ref,
           ag_ref, send1_ref, a2s_ref, a2r_ref, pick_ref, spread_ref,
           hi_ref, his_ref, hj_ref, hjs_ref, cs_ref, cr_ref,
           dsem, ag_s, ag_r, a2_s, a2_r, h_s, h_r, c_s, c_r):
    n = nsub * ncg
    s = lax.axis_index("sub")
    t = lax.axis_index("cgrp")
    me = s * ncg + t

    def peer(o):
        d = lax.rem(me + o, n)
        return d, (lax.div(d, ncg), lax.rem(d, ncg))

    early = []
    for k, (src, dst) in enumerate(((face_any, face_ref), (map_any, map_ref), (x_any, x_ref),
                                    (modes_any, modes_ref), (cols_any, cols_ref),
                                    (wt_any, w_ref), (blk_any, blk_ref), (cap_any, cap_ref))):
        early.append(pltpu.make_async_copy(src, dst, dsem.at[k]))
        early[-1].start()
    fcopy, mcopy, xcopy, ocopy, lcopy, wcopy, bcopy, ccopy = early

    def peers(step):
        if n > 32:
            pl.loop(1, n)(step)
        else:
            for o in range(1, n):
                step(o)

    barrier = pltpu.get_barrier_semaphore()

    @pl.loop(1, n)
    def _(o):
        _, dev = peer(o)
        pl.semaphore_signal(barrier, inc=1, device_id=dev, device_id_type=MESH)

    lane = iota((1, 128), 1)
    low = lane < 64
    low32 = jnp.broadcast_to(low, (32, 128))
    low64 = jnp.broadcast_to(low, (64, 128))

    def swap(a):
        return pltpu.roll(a, 64, 1)

    @pl.loop(0, 8)
    def _(c):
        r = iota((128, 512), 0)
        col = iota((128, 512), 1) + c * 512
        hit = ((col >> 6) == (r & 63)) & ((col & 63) == 63 * (r >> 6))
        sel_ref[:, pl.ds(pl.multiple_of(c * 512, 512), 512)] = jnp.where(hit, 1.0, 0.0).astype(bf16)

    fcopy.wait()
    mcopy.wait()
    fm0t = face_ref[0]
    fm1t = face_ref[1]
    r64 = iota((64, 64), 0)
    c64 = iota((64, 64), 1)
    eye64 = jnp.where(r64 == c64, 1.0, 0.0)
    qm = jnp.where(c64 == 2 * (r64 & 31) + (r64 >> 5), 1.0, 0.0)
    dup = jnp.where((iota((64, 128), 1) & 63) == iota((64, 128), 0), 1.0, 0.0)
    dupt = jnp.where((iota((128, 64), 0) & 63) == iota((128, 64), 1), 1.0, 0.0)
    eye128 = jnp.where(iota((128, 128), 0) == iota((128, 128), 1), 1.0, 0.0)
    fm0pt = nn(qm, fm0t)
    fm0 = fm0t.T
    fm0p = fm0pt.T
    fm11 = jnp.concatenate([fm1t, fm1t], axis=0).T

    mapf = [(map_ref[f] & 127).astype(f32) for f in range(6)]
    mapf = jnp.concatenate(mapf + [jnp.zeros((2, 128), f32)], axis=0)
    mapt = mmt(eye128.astype(bf16), mapf.astype(bf16))
    lanef = iota((128, 128), 1).astype(f32)

    xcopy.wait()
    for q in range(T):
        s_ref[q * 8 : q * 8 + 8, :] = x_ref[0:8, q * 128 : q * 128 + 128]
        s_ref[256 + q * 8 : 256 + q * 8 + 8, :] = x_ref[56:64, q * 128 : q * 128 + 128]
    y0 = s_ref[pl.ds(0, 32, stride=8), :]
    y1 = s_ref[pl.ds(263, 32, stride=8), :]
    f01 = jnp.concatenate([jnp.where(low32, y0, swap(y1)), jnp.where(low32, swap(y0), y1)], axis=0)
    f23 = jnp.where(low64, x_ref[:, :128], x_ref[:, 31 * 128 :])
    xh, xl = split(x_ref[...])
    f45 = mmt(jnp.concatenate([xh, xl], axis=0), sel_ref[...])
    f45 = f45[:64] + f45[64:]

    rows = []
    for pair, (left, plane) in enumerate(((fm0p, f01), (fm0, f23), (fm0, f45))):
        u = mm(left3(left), rows3(plane)) * fm11
        for half in range(2):
            keep = low if half == 0 else jnp.logical_not(low)
            val = jnp.sum(jnp.where(keep, u, 0.0), axis=1, keepdims=True)
            f = 2 * pair + half
            place = mapt[:, f : f + 1] == lanef
            rows.append(jnp.sum(jnp.where(place, val, 0.0), axis=0, keepdims=True))
    mine = jnp.concatenate(rows + [jnp.zeros((2, 128), f32)], axis=0)
    send1_ref[...] = mine
    ag_ref[me] = mine

    pl.semaphore_wait(barrier, n - 1)

    @peers
    def _(o):
        _, dev = peer(o)
        pltpu.make_async_remote_copy(src_ref=send1_ref, dst_ref=ag_ref.at[me], send_sem=ag_s, recv_sem=ag_r,
                                     device_id=dev, device_id_type=MESH).start()

    ocopy.wait()
    m0, m1, m2 = modes_ref[0], modes_ref[1], modes_ref[2]
    am_ref[0] = left3(m0)
    am_ref[1] = left3(nt(eye64, m0))
    am_ref[2] = left3(nt(nn(qm, m1), qm))
    am_ref[3] = left3(nt(nt(qm, m1), qm))
    block = (iota((128, 128), 0) >> 6) == (iota((128, 128), 1) >> 6)
    kw_ref[0] = lanes_weights(jnp.where(block, nn(nt(dupt, m2), dup), 0.0))
    kw_ref[1] = lanes_weights(jnp.where(block, nn(dupt, nn(m2, dup)), 0.0))

    @pl.loop(0, T // CH)
    def _(c):
        base = pl.multiple_of(c * (CH * 128), CH * 128)
        y = mm(am_ref[0], rows3(x_ref[:, pl.ds(base, CH * 128)]))
        stacked = jnp.concatenate([y[:, g * 128 : g * 128 + 128] for g in range(CH)], axis=0)
        s_ref[pl.ds(pl.multiple_of(c * (CH * 64), CH * 64), CH * 64), :] = lane_transform(stacked, kw_ref[0])

    wcopy.wait()
    for q in range(T):
        z_ref[q * 64 : q * 64 + 64, :] = w_ref[:, q * 128 : q * 128 + 128]

    def turned(ref, u):
        a = ref[pl.ds(u, 32, stride=64), :]
        b = ref[pl.ds(u + 32, 32, stride=64), :]
        return jnp.concatenate([jnp.where(low32, a, swap(b)), jnp.where(low32, swap(a), b)], axis=0)

    def middle(c, acc):
        fwd = jnp.concatenate([turned(s_ref, c * CH + g) for g in range(CH)], axis=1)
        wts = jnp.concatenate([turned(z_ref, c * CH + g) for g in range(CH)], axis=1)
        v = mm(am_ref[2], rows3(fwd))
        wv = wts * v
        prod = wv * v
        for g in range(CH):
            acc = acc + prod[:, g * 128 : g * 128 + 128]
        y = mm(am_ref[3], rows3(wv))
        for g in range(CH):
            p_ref[pl.ds(pl.multiple_of(64 + (c * CH + g) * 64, 64), 64), :] = y[:, g * 128 : g * 128 + 128]
        return acc

    gacc = lax.fori_loop(0, T // CH // 2, middle, jnp.zeros((64, 128), f32))

    lcopy.wait()
    cols = cols_ref[...]
    nrow = cols.shape[0]
    nz = cols.shape[1]
    wide_cols = jnp.concatenate([jnp.broadcast_to(cols[i : i + 1, :], (nz, nz)) for i in range(nrow)], axis=0)
    kk = nrow * nz
    pick_diag = iota((kk, nz), 1) == (iota((kk, nz), 0) & (nz - 1))
    colv = jnp.sum(jnp.where(pick_diag, wide_cols.astype(f32), 0.0), axis=1, keepdims=True)
    r = iota((1, n * 8), 1)
    d = r >> 3
    f = r & 7
    own = nrow * d + f
    own = jnp.where((f == 0) & (d >= ncg), nrow * (d - ncg) + 1, own)
    own = jnp.where((f == 2) & (lax.rem(d, ncg) > 0), nrow * (d - 1) + 3, own)
    own = jnp.where(f >= 6, -1, own).astype(f32)
    g1 = jnp.where(colv == own, 1.0, 0.0)
    g1 = jnp.concatenate([g1, jnp.zeros((128 - kk, n * 8), f32)], axis=0)

    g2 = g1.T.astype(bf16)
    g2 = jnp.concatenate([g2, g2], axis=1)
    g1 = g1.astype(bf16)

    pltpu.make_async_copy(ag_ref.at[pl.ds(0, n - 1)], ag_ref.at[pl.ds(0, n - 1)], ag_r).wait()
    th, tl = split(ag_ref[...].reshape(n * 8, 128))
    picked = mm(g1, th) + mm(g1, tl)
    pick_ref[...] = picked[:kk].reshape(nrow, nz, 128)
    bcopy.wait()
    spread_ref[...] = jnp.zeros_like(spread_ref)

    def coarse_row(i, acc):
        pk = pick_ref[i]
        tot = blk_ref[i, 0] * pk[0:1]
        for k in range(1, nz):
            tot = tot + blk_ref[i, k] * pk[k : k + 1]
        img = jnp.sum(tot, axis=1, keepdims=True)
        out = [jnp.sum(blk_ref[i, k] * img, axis=0, keepdims=True) for k in range(nz)]
        spread_ref[i] = jnp.concatenate(out, axis=0)
        return acc + img * img

    iacc = lax.fori_loop(0, nrow, coarse_row, jnp.zeros((128, 1), f32))
    back = mm(g2, jnp.concatenate(split(spread_ref[...].reshape(128, 128)), axis=0))
    a2s_ref[...] = back.reshape(n, 8, 128)
    a2r_ref[me] = a2s_ref[me]

    @peers
    def _(o):
        dd, dev = peer(o)
        pltpu.make_async_remote_copy(src_ref=a2s_ref.at[dd], dst_ref=a2r_ref.at[me], send_sem=a2_s, recv_sem=a2_r,
                                     device_id=dev, device_id_type=MESH).start()

    gacc = lax.fori_loop(T // CH // 2, T // CH, middle, gacc)
    gpart = jnp.sum(iacc, keepdims=True) + jnp.sum(gacc, keepdims=True)

    @pl.loop(0, T // CH)
    def _(c):
        tiles = []
        for g in range(CH):
            a = p_ref[pl.ds(64 + c * CH + g, 32, stride=64), :]
            b = p_ref[pl.ds(96 + c * CH + g, 32, stride=64), :]
            tiles.append(jnp.where(low32, a, swap(b)))
            tiles.append(jnp.where(low32, swap(a), b))
        k = lane_transform(jnp.concatenate(tiles, axis=0), kw_ref[1])
        y = jnp.concatenate([k[g * 64 : g * 64 + 64] for g in range(CH)], axis=1)
        y = mm(am_ref[1], rows3(y))
        for g in range(CH):
            s_ref[pl.ds(pl.multiple_of((c * CH + g) * 64, 64), 64), :] = y[:, g * 128 : g * 128 + 128]

    pltpu.make_async_copy(a2r_ref.at[pl.ds(0, n - 1)], a2r_ref.at[pl.ds(0, n - 1)], a2_r).wait()
    backs = jnp.sum(a2r_ref[...], axis=0)
    corr = []
    for f in range(6):
        place = mapt[:, f : f + 1] == lanef
        corr.append(jnp.sum(jnp.where(place, backs[f : f + 1], 0.0), axis=1, keepdims=True))
    e01 = mm(left3(fm0pt), rows3(jnp.where(low, corr[0], corr[1]) * fm11))
    e23 = mm(left3(fm0t), rows3(jnp.where(low, corr[2], corr[3]) * fm11))
    e45 = mm(left3(fm0t), rows3(jnp.where(low, corr[4], corr[5]) * fm11))
    eh, el = split(e45)
    eh = jnp.concatenate([eh, el], axis=0)

    @pl.loop(0, T // CH)
    def _(c):
        base = pl.multiple_of(c * (CH * 128), CH * 128)
        add = mm(eh, sel_ref[:, pl.ds(base, CH * 128)])
        for g in range(CH):
            at = pl.multiple_of((c * CH + g) * 64, 64)
            tile = add[:64, g * 128 : g * 128 + 128] + add[64:, g * 128 : g * 128 + 128]
            p_ref[pl.ds(at + 64, 64), :] = s_ref[pl.ds(at, 64), :] + tile

    p_ref[64:128, :] += jnp.where(low64, e23, 0.0)
    p_ref[T * 64 : T * 64 + 64, :] += jnp.where(low64, 0.0, e23)
    top, bottom = e01[:32], e01[32:]
    edge0 = p_ref[pl.ds(64, 32, stride=64), :] + jnp.where(low32, top, swap(bottom))
    edge1 = p_ref[pl.ds(64 + 63, 32, stride=64), :] + jnp.where(low32, swap(top), bottom)
    p_ref[pl.ds(64, 32, stride=64), :] = edge0
    p_ref[pl.ds(64 + 63, 32, stride=64), :] = edge1

    his_ref[0] = edge0
    his_ref[1] = edge1
    hjs_ref[0] = p_ref[64:128, :]
    hjs_ref[1] = p_ref[T * 64 : T * 64 + 64, :]

    sends = (
        (s > 0, s < nsub - 1, (s - 1, t), his_ref, hi_ref, 0, 1, 0),
        (s < nsub - 1, s > 0, (s + 1, t), his_ref, hi_ref, 1, 0, 1),
        (t > 0, t < ncg - 1, (s, t - 1), hjs_ref, hj_ref, 0, 1, 2),
        (t < ncg - 1, t > 0, (s, t + 1), hjs_ref, hj_ref, 1, 0, 3),
    )

    def halo(dev, src, dst, a, b, k):
        return pltpu.make_async_remote_copy(src_ref=src.at[a], dst_ref=dst.at[b], send_sem=h_s.at[k],
                                            recv_sem=h_r.at[k], device_id=dev, device_id_type=MESH)

    for does, gets, dev, src, dst, a, b, k in sends:
        @pl.when(does)
        def _():
            halo(dev, src, dst, a, b, k).start()

        @pl.when(jnp.logical_not(gets))
        def _():
            dst[b] = jnp.zeros(dst.shape[1:], f32)

    ccopy.wait()
    p_ref[0:64, :] = jnp.zeros((64, 128), f32)
    p_ref[(T + 1) * 64 : (T + 2) * 64, :] = jnp.zeros((64, 128), f32)

    row = iota((64, 128), 0)
    kpos = iota((64, 128), 1) & 63

    def stencil(q, acc):
        at = pl.multiple_of(q * 64, 64)
        x = p_ref[pl.ds(at + 64, 64), :]
        here = swap(x)
        before = swap(p_ref[pl.ds(at, 64), :])
        after = swap(p_ref[pl.ds(at + 128, 64), :])
        second = here + jnp.where(low64, before, after)
        up = jnp.where(row == 0, 0.0, pltpu.roll(x, 1, 0))
        down = jnp.where(row == 63, 0.0, pltpu.roll(x, 63, 0))
        third = jnp.where(kpos == 0, 0.0, pltpu.roll(x, 1, 1)) + jnp.where(kpos == 63, 0.0, pltpu.roll(x, 127, 1))
        cols_at = pl.ds(pl.multiple_of(q * 128, 128), 128)
        img = (cap_ref[:, cols_at] + 8.2) * x - (up + down) - 0.6 * second - 2.5 * third
        img_out[:, cols_at] = img
        p_out[:, cols_at] = x
        return acc + x * img

    cacc = lax.fori_loop(0, T, stencil, jnp.zeros((64, 128), f32), unroll=2)
    for does, gets, dev, src, dst, a, b, k in sends:
        @pl.when(gets)
        def _():
            halo(dev, src, dst, a, b, k).wait_recv()

    fix0 = 0.6 * jnp.where(low64, swap(hj_ref[0]), 0.0)
    fix1 = 0.6 * jnp.where(low64, 0.0, swap(hj_ref[1]))
    cacc = cacc - hjs_ref[0] * fix0 - hjs_ref[1] * fix1
    csum = his_ref[0] * hi_ref[0] + his_ref[1] * hi_ref[1]
    cpart = jnp.sum(cacc, axis=0, keepdims=True) - jnp.sum(csum, axis=0, keepdims=True)
    cpart = jnp.where(low, cpart + swap(cpart), gpart * (1.0 / 64.0))
    cs_ref[...] = cpart
    cr_ref[me] = cpart

    @peers
    def _(o):
        _, dev = peer(o)
        pltpu.make_async_remote_copy(src_ref=cs_ref, dst_ref=cr_ref.at[me], send_sem=c_s, recv_sem=c_r,
                                     device_id=dev, device_id_type=MESH).start()

    img_out[:, :128] = img_out[:, :128] - fix0
    img_out[:, (T - 1) * 128 :] = img_out[:, (T - 1) * 128 :] - fix1
    for q in range(T):
        at = slice(q * 128, q * 128 + 128)
        img_out[0:1, at] = img_out[0:1, at] - hi_ref[0, q : q + 1, :]
        img_out[63:64, at] = img_out[63:64, at] - hi_ref[1, q : q + 1, :]

    pltpu.make_async_copy(cr_ref.at[pl.ds(0, n - 1)], cr_ref.at[pl.ds(0, n - 1)], c_r).wait()
    both = jnp.sum(cr_ref[...], axis=0)
    curv = jnp.sum(jnp.where(low, both, 0.0), axis=1, keepdims=True)
    gamma = jnp.sum(jnp.where(low, 0.0, both), axis=1, keepdims=True)
    alpha_out[...] = gamma / curv

    pltpu.make_async_copy(ag_ref.at[pl.ds(0, n - 1)], ag_ref.at[pl.ds(0, n - 1)], ag_s).wait()
    pltpu.make_async_copy(a2r_ref.at[pl.ds(0, n - 1)], a2r_ref.at[pl.ds(0, n - 1)], a2_s).wait()
    pltpu.make_async_copy(cr_ref.at[pl.ds(0, n - 1)], cr_ref.at[pl.ds(0, n - 1)], c_s).wait()
    for does, gets, dev, src, dst, a, b, k in sends:
        @pl.when(does)
        def _():
            halo(dev, src, dst, a, b, k).wait_send()


def body(nsub, ncg, source, capacity, fd_weights, fd_modes, face_modes, coarse_map, fsai_cols, fsai_blocks):
    n = nsub * ncg
    nrow, nz = fsai_cols.shape
    vm = pl.BlockSpec(memory_space=pltpu.VMEM)
    hbm = pl.BlockSpec(memory_space=pltpu.HBM)
    field = jax.ShapeDtypeStruct(source.shape, f32)
    V = pltpu.VMEM
    dma = pltpu.SemaphoreType.DMA
    p, img, alpha = pl.pallas_call(
        functools.partial(kernel, nsub, ncg),
        out_shape=(field, field, jax.ShapeDtypeStruct((1, 1), f32)),
        in_specs=[hbm] * 8,
        out_specs=(vm, vm, vm),
        scratch_shapes=[
            V(source.shape, f32),
            V(fd_modes.shape, f32),
            V((2, 64, 128), f32),
            V((6, 1, 128), jnp.int32),
            V(fsai_cols.shape, jnp.int32),
            V((T * 64, 128), f32),
            V((T * 64, 128), f32),
            V((64, T * 128), f32),
            V(((T + 2) * 64, 128), f32),
            V((64, T * 128), f32),
            V(fsai_blocks.shape, f32),
            V((128, T * 128), bf16),
            V((4, 64, 192), bf16),
            V((2, 256, 256), bf16),
            V((n, 8, 128), f32),
            V((8, 128), f32),
            V((n, 8, 128), f32),
            V((n, 8, 128), f32),
            V((nrow, nz, 128), f32),
            V((128 // nz, nz, 128), f32),
            V((2, 32, 128), f32),
            V((2, 32, 128), f32),
            V((2, 64, 128), f32),
            V((2, 64, 128), f32),
            V((1, 128), f32),
            V((n, 1, 128), f32),
            dma((8,)),
            dma, dma, dma, dma,
            dma((4,)), dma((4,)),
            dma, dma,
        ],
        compiler_params=pltpu.CompilerParams(collective_id=0, has_side_effects=True,
                                             vmem_limit_bytes=48 * 1024 * 1024),
        cost_estimate=pl.CostEstimate(flops=10**9, bytes_accessed=8 * 2**20, transcendentals=0),
        name="step",
    )(*(pltpu.with_memory_space_constraint(v, pltpu.HBM) for v in (
        source, fd_modes, jnp.swapaxes(face_modes, 1, 2), coarse_map.reshape(-1, 1, coarse_map.shape[-1]),
        fsai_cols, capacity, fd_weights, fsai_blocks)))
    a = alpha[0, 0]
    return a * p, source - a * img


def solution(mesh):
    in_specs = (
        P("sub", "cgrp"),
        P("sub", "cgrp"),
        P("sub", "cgrp"),
        P(),
        P(),
        P("sub", "cgrp", None, None),
        P(("sub", "cgrp"), None),
        P(("sub", "cgrp"), None, None, None),
    )
    out_specs = (P("sub", "cgrp"), P("sub", "cgrp"))
    step = functools.partial(body, mesh.shape["sub"], mesh.shape["cgrp"])
    return jax.shard_map(step, mesh=mesh, in_specs=in_specs, out_specs=out_specs, check_vma=False)
```
